32 devices in a mesh: sample: 4 (over z), space: 8 (over y, x, core).
Axes of the slice: x: 2, y: 2, z: 4, core: 2. Of those that a mesh axis runs over, the one named last changes fastest.
Arguments:
- concentration: float32 [4, 4, 512, 512], P('sample', None, 'space'), may hold values from -12 to 12
- classes: int32 [4, 4, 512, 512], P('sample', None, 'space'), may hold values from 0 to 15
- conductivity: float32 [16], replicated, may hold values from 0.1 to 10
- wells: int32 [2, 64], replicated, may hold values from 0 to 511
- control: float32 [64], replicated, may hold values from -40 to 40
Outputs:
- final_conc: float32 [4, 4, 512, 512], P('sample', None, 'space')
- adjoint_start: float32 [4, 4, 512, 512], P('sample', None, 'space')
- gradient: float32 [64], replicated
The draws below stay inside these ranges and needn't reach their ends.
All inputs are finite; a program needn't handle non-finite values.
Results may differ from the reference program's by a relative error of at most 0.0003.
Values sent between devices are 32-bit elements; how exact they have to be, the bound alone decides.
A program may use at most 128 MiB of HBM per device.

```python
import math
import jax
import jax.numpy as jnp
from jax import lax

GRID = 512
NZ = 4
CLASSES = 16
WELLS = 64
SAMPLES = 4


def with_ends(result, key, smallest, top_value):
    shape = result.shape
    place = [jax.random.randint(jax.random.fold_in(key, axis), (), 0, shape[axis]) for axis in range(len(shape))]
    result = result.at[tuple(place)].set(smallest)
    longest = shape.index(max(shape))
    place[longest] = (place[longest] + 1) % shape[longest]
    return result.at[tuple(place)].set(top_value)


def shard_levels(own_key, dims, pieces, smallest, high):
    def one(axis_at, blocks):
        heights = jax.random.uniform(jax.random.fold_in(jax.random.fold_in(own_key, 6), axis_at), (blocks,), jnp.float32, smallest / len(pieces), high / len(pieces))
        return jnp.repeat(jnp.exp(heights), dims[axis_at] // blocks).reshape((-1,) + (1,) * (len(dims) - axis_at - 1))

    gain = one(*pieces[0])
    for cut in pieces[1:]:
        gain = gain * one(*cut)
    return gain


def centred(stream_key, shape, scale, reach, shards=(), kind=jnp.bfloat16):
    level = shard_levels(stream_key, shape, shards, -0.22, 0.18) if shards else 1.0
    values = jax.random.normal(stream_key, shape, jnp.float32) * scale * level
    return jnp.minimum(jnp.maximum(values, -reach), reach).astype(kind)


def setup_inputs(seed: int = 0) -> dict:
    keys = jax.random.split(jax.random.key(seed), 6)
    concentration = centred(keys[0], (SAMPLES, NZ, GRID, GRID), 2.0, 12.0, ((0, 4), (2, 8)), jnp.float32)
    classes = with_ends(jax.random.randint(keys[1], (SAMPLES, NZ, GRID, GRID), 0, CLASSES), jax.random.fold_in(keys[1], 1), 0, CLASSES - 1).astype(jnp.int32)
    conductivity = jnp.clip(jnp.exp(jax.random.uniform(keys[2], (CLASSES,), jnp.float32, math.log(0.1), math.log(10.0))), 0.1, 10.0)
    wells = with_ends(jax.random.randint(keys[3], (2, WELLS), 0, GRID), jax.random.fold_in(keys[3], 1), 0, GRID - 1).astype(jnp.int32)
    control = jnp.clip(jax.random.uniform(keys[4], (WELLS,), jnp.float32, -40.0, 40.0), -40.0, 40.0)
    return {"concentration": concentration, "classes": classes, "conductivity": conductivity, "wells": wells, "control": control}


spread_along = 200.0
drift_along = 6.0
spread_across = 200.0
drift_across = 3.0
spread_depth = 2.0
drift_depth = 0.0
aversion = 0.5
epsilon = 1e-06

def line_terms(conduct, spread, advection):
    harmonic = 2.0 * conduct[..., :-1] * conduct[..., 1:] / (conduct[..., :-1] + conduct[..., 1:])
    zeros_edge = jnp.zeros(conduct.shape[:-1] + (1,), conduct.dtype)
    behind = jnp.concatenate([zeros_edge, harmonic], axis=-1)
    face_ahead = jnp.concatenate([harmonic, zeros_edge], axis=-1)
    subdiag = -(spread * behind + advection)
    subdiag = jnp.concatenate([zeros_edge, subdiag[..., 1:]], axis=-1)
    middle = 1.0 + spread * (behind + face_ahead) + advection
    superdiag = -spread * face_ahead
    return (subdiag, middle, superdiag)

def solve_lines(quantity, conduct, direction, spread, advection, transposed):
    lines_last = jnp.moveaxis(quantity, direction, -1)
    subdiag, middle, superdiag = line_terms(jnp.moveaxis(conduct, direction, -1), spread, advection)
    if transposed:
        zeros_edge = jnp.zeros(subdiag.shape[:-1] + (1,), subdiag.dtype)
        new_sub = jnp.concatenate([zeros_edge, superdiag[..., :-1]], axis=-1)
        new_super = jnp.concatenate([subdiag[..., 1:], zeros_edge], axis=-1)
        subdiag, superdiag = (new_sub, new_super)
    solution = lax.linalg.tridiagonal_solve(subdiag, middle, superdiag, lines_last[..., None])[..., 0]
    return jnp.moveaxis(solution, -1, direction)

def reference(concentration, classes, conductivity, wells, control):
    source = jnp.zeros((GRID, GRID), jnp.float32).at[wells[0], wells[1]].add(control)
    finals = []
    adjoints = []
    misfits = []
    well_terms = []
    for sample in range(SAMPLES):
        conduct = conductivity[classes[sample]]
        current = concentration[sample] + source[None]
        current = solve_lines(current, conduct, 1, spread_along, drift_along, False)
        current = solve_lines(current, conduct, 0, spread_depth, drift_depth, False)
        current = solve_lines(current, conduct, 2, spread_across, drift_across, False)
        current = current + source[None]
        current = solve_lines(current, conduct, 2, spread_across, drift_across, False)
        current = solve_lines(current, conduct, 0, spread_depth, drift_depth, False)
        current = solve_lines(current, conduct, 1, spread_along, drift_along, False)
        second_adjoint = solve_lines(current, conduct, 1, spread_along, drift_along, True)
        second_adjoint = solve_lines(second_adjoint, conduct, 0, spread_depth, drift_depth, True)
        second_adjoint = solve_lines(second_adjoint, conduct, 2, spread_across, drift_across, True)
        first_adjoint = solve_lines(second_adjoint, conduct, 2, spread_across, drift_across, True)
        first_adjoint = solve_lines(first_adjoint, conduct, 0, spread_depth, drift_depth, True)
        first_adjoint = solve_lines(first_adjoint, conduct, 1, spread_along, drift_along, True)
        misfits.append(0.5 * jnp.sum(current * current))
        column_total = jnp.sum(second_adjoint + first_adjoint, axis=0)
        well_terms.append(column_total[wells[0], wells[1]])
        finals.append(jnp.transpose(current, (0, 2, 1)))
        adjoints.append(jnp.transpose(first_adjoint, (0, 2, 1)))
    misfit = jnp.stack(misfits)
    average = jnp.sum(misfit) / SAMPLES
    weights = (1.0 + aversion * (misfit - average) / (average + epsilon)) / SAMPLES
    gradient = jnp.sum(weights[:, None] * jnp.stack(well_terms), axis=0)
    return (jnp.stack(finals), jnp.stack(adjoints), gradient)
```

```python
import functools
import jax
import jax.numpy as jnp
from jax import lax
from jax.experimental import pallas as pl
from jax.experimental.pallas import tpu as pltpu
from jax.sharding import PartitionSpec as P

spread_along = 200.0
drift_along = 6.0
spread_across = 200.0
drift_across = 3.0
spread_depth = 2.0
drift_depth = 0.0
aversion = 0.5
epsilon = 1e-06


def offset(values, amount, direction, filler):
    length = values.shape[direction]
    distance = abs(amount)
    margin = list(values.shape)
    margin[direction] = distance
    padding = jnp.full(margin, filler, values.dtype)
    if amount > 0:
        retained = lax.slice_in_dim(values, 0, length - distance, axis=direction)
        return jnp.concatenate([padding, retained], axis=direction)
    retained = lax.slice_in_dim(values, distance, length, axis=direction)
    return jnp.concatenate([retained, padding], axis=direction)


def line_terms(conduct, direction, spread, advection):
    following = offset(conduct, -1, direction, 0.0)
    face_ahead = 2.0 * conduct * following / (conduct + following)
    behind = offset(face_ahead, 1, direction, 0.0)
    subdiag = offset(-(spread * face_ahead + advection), 1, direction, 0.0)
    middle = 1.0 + spread * (behind + face_ahead) + advection
    superdiag = -spread * face_ahead
    return (subdiag, middle, superdiag)


def factor_lines(terms, direction):
    subdiag, middle, superdiag = terms
    length = middle.shape[direction]
    levels = []
    stride = 1
    while stride < length:
        middle_before = offset(middle, stride, direction, 1.0)
        middle_after = offset(middle, -stride, direction, 1.0)
        weight_below = -subdiag / middle_before
        weight_above = -superdiag / middle_after
        new_middle = (
            middle
            + weight_below * offset(superdiag, stride, direction, 0.0)
            + weight_above * offset(subdiag, -stride, direction, 0.0)
        )
        subdiag = weight_below * offset(subdiag, stride, direction, 0.0)
        superdiag = weight_above * offset(superdiag, -stride, direction, 0.0)
        middle = new_middle
        levels.append((weight_below, weight_above))
        stride = stride * 2
    return (levels, middle)


def solve_lines(values, factored, direction):
    levels, middle = factored
    stride = 1
    for weight_below, weight_above in levels:
        values = (
            values
            + weight_below * offset(values, stride, direction, 0.0)
            + weight_above * offset(values, -stride, direction, 0.0)
        )
        stride = stride * 2
    return values / middle


def solve_back(values, factored, direction):
    levels, middle = factored
    values = values / middle
    for depth_level in range(len(levels) - 1, -1, -1):
        weight_below, weight_above = levels[depth_level]
        stride = 2**depth_level
        values = (
            values
            + offset(weight_below * values, -stride, direction, 0.0)
            + offset(weight_above * values, stride, direction, 0.0)
        )
    return values


def pack_lines(values):
    planes, rows_here, length = values.shape
    count = lax.axis_size("space")
    return values.reshape(planes, rows_here, count, length // count).transpose(0, 2, 3, 1)


def unpack_lines(values):
    return values.reshape(values.shape[0], values.shape[2], values.shape[3])


def into_columns(values):
    return unpack_lines(
        lax.all_to_all(pack_lines(values), "space", split_axis=1, concat_axis=3, tiled=True)
    )


def into_rows(values):
    return unpack_lines(
        lax.all_to_all(pack_lines(values), "space", split_axis=1, concat_axis=3, tiled=True)
    )


def well_sum(column_sum, hits_rows, hits_columns):
    picked = jnp.dot(
        hits_rows, column_sum, precision=lax.Precision.HIGHEST, preferred_element_type=jnp.float32
    )
    return jnp.sum(picked * hits_columns, axis=1)


def per_device(concentration, classes, conductivity, wells, control):
    start_state = concentration[0]
    class_cells = classes[0]
    grid_cells = start_state.shape[2]
    block_size = start_state.shape[1]
    position = lax.axis_index("space")
    conduct_rows = jnp.zeros(class_cells.shape, jnp.float32)
    for class_label in range(conductivity.shape[0]):
        conduct_rows = conduct_rows + jnp.where(
            class_cells == class_label, conductivity[class_label], 0.0
        )
    conduct_columns = unpack_lines(
        lax.all_to_all(pack_lines(conduct_rows), "space", split_axis=1, concat_axis=3, tiled=True)
    )
    along_factor = factor_lines(line_terms(conduct_columns, 2, spread_along, drift_along), 2)
    across_factor = factor_lines(line_terms(conduct_rows, 2, spread_across, drift_across), 2)
    depth_rows = factor_lines(line_terms(conduct_rows, 0, spread_depth, drift_depth), 0)
    local_index = position * block_size + lax.iota(jnp.int32, block_size)
    all_index = lax.iota(jnp.int32, grid_cells)
    hits_first_local = (wells[0][:, None] == local_index[None, :]).astype(jnp.float32)
    hits_second_all = (wells[1][:, None] == all_index[None, :]).astype(jnp.float32)
    hits_second_local = (wells[1][:, None] == local_index[None, :]).astype(jnp.float32)
    hits_first_all = (wells[0][:, None] == all_index[None, :]).astype(jnp.float32)
    source = jnp.dot(
        hits_first_local.T,
        control[:, None] * hits_second_all,
        precision=lax.Precision.HIGHEST,
        preferred_element_type=jnp.float32,
    )
    depth_columns = factor_lines(line_terms(conduct_columns, 0, spread_depth, drift_depth), 0)
    current = into_columns(start_state + source[None])
    current = solve_lines(current, along_factor, 2)
    current = solve_lines(current, depth_columns, 0)
    current = into_rows(current)
    current = solve_lines(current, across_factor, 2)
    current = current + source[None]
    current = solve_lines(current, across_factor, 2)
    current = solve_lines(current, depth_rows, 0)
    final_state = solve_lines(into_columns(current), along_factor, 2)
    misfit_part = 0.5 * jnp.sum(final_state * final_state)
    second_adjoint = solve_back(final_state, along_factor, 2)
    second_adjoint = solve_back(second_adjoint, depth_columns, 0)
    second_adjoint = solve_back(into_rows(second_adjoint), across_factor, 2)
    first_adjoint = solve_back(second_adjoint, across_factor, 2)
    first_adjoint = solve_back(first_adjoint, depth_rows, 0)
    adjoint_state = solve_back(into_columns(first_adjoint), along_factor, 2)
    well_terms = well_sum(jnp.sum(second_adjoint, axis=0), hits_first_local, hits_second_all)
    well_terms = well_terms + well_sum(
        jnp.sum(adjoint_state, axis=0), hits_second_local, hits_first_all
    )
    sample_count = lax.axis_size("sample")
    own_misfit = lax.psum(misfit_part, "space")
    misfit_total = lax.psum(own_misfit, "sample")
    average = misfit_total / sample_count
    weight = (1.0 + aversion * (own_misfit - average) / (average + epsilon)) / sample_count
    gradient = lax.psum(weight * well_terms, ("sample", "space"))
    return (final_state[None], adjoint_state[None], gradient)


LANES = 128
SUBLANES = 8
UNROLL = 8
MESH = pl.DeviceIdType.MESH
EXACT = lax.Precision.HIGHEST


def steps(count, body, carry):
    def turn(t, state):
        for k in range(UNROLL):
            state = body(t * UNROLL + k, state)
        return state

    return lax.fori_loop(0, count // UNROLL, turn, carry)


def rows_at(i, pieces, length):
    return pl.ds(i, pieces, stride=length)


def take(ref, at):
    return jnp.concatenate([ref[j, at, :] for j in range(ref.shape[0])], axis=1)


def put(ref, at, value):
    for j in range(ref.shape[0]):
        ref[j, at, :] = value[:, j * LANES : (j + 1) * LANES]


def width(ref):
    return ref.shape[0] * LANES


def factor_blocks(cond, factors, pieces, length, before, beyond, spread, drift):
    low, up, inv, from_first, to_first = factors
    shape = (pieces, width(cond))

    def keep(i, d, ahead, state):
        eta, eta_t, corner = state
        r = 1.0 / d
        u = -spread * ahead * r
        lo = -(spread * ahead + drift) * r
        at = rows_at(i, pieces, length)
        put(low, at, lo)
        put(up, at, u)
        put(inv, at, r)
        first = eta * r
        put(from_first, at, first)
        put(to_first, at, eta_t * r)
        return u, (-lo * eta, -u * eta_t, corner + first * eta_t)

    def body(i, state):
        here, behind, u, rest = state
        after = take(cond, rows_at(jnp.minimum(i + 1, length - 1), pieces, length))
        ahead = 2.0 * here * after / (here + after)
        ahead = jnp.where(i == length - 1, last_face, ahead)
        d = 1.0 + spread * (behind + ahead) + drift + (spread * behind + drift) * u
        u, rest = keep(i, d, ahead, rest)
        return after, ahead, u, rest

    first_row = take(cond, rows_at(0, pieces, length))
    last_face = beyond(first_row, take(cond, rows_at(length - 1, pieces, length)))
    ones = jnp.ones(shape, jnp.float32)
    zeros = jnp.zeros(shape, jnp.float32)
    state = steps(length, body, (first_row, before, zeros, (ones, ones, zeros)))
    at = rows_at(length - 1, pieces, length)
    return state[3][2], take(from_first, at), take(to_first, at), take(inv, at), last_face


def sweep_down(values, out, low, inv, weights, pieces, length):
    def body(i, state):
        y, lo, total = state
        at = rows_at(i, pieces, length)
        y = take(values, at) - lo * y
        put(out, at, y * take(inv, at))
        return y, take(low, at), total + take(weights, at) * y

    zeros = jnp.zeros((pieces, width(values)), jnp.float32)
    _, _, total = steps(length, body, (zeros, zeros, zeros))
    return total, take(out, rows_at(length - 1, pieces, length))


def sweep_up(held, out, up, spike, incoming, following, pieces, length):
    def body(k, x):
        at = rows_at(length - 1 - k, pieces, length)
        x = take(held, at) - take(spike, at) * incoming - take(up, at) * x
        put(out, at, x)
        return x

    steps(length, body, following)


def joint_terms(vf, vl, wf, wl, beta):
    r = 1.0 / (1.0 - vf * beta)
    s = vl * beta * r
    return s, vl + s * vf, r, r * vf, r * wf, wl + s * wf


def tile_transpose(source, target):
    for i in range(target.shape[0]):
        for j in range(source.shape[0]):
            target[i, j * LANES : (j + 1) * LANES, :] = source[j, i * LANES : (i + 1) * LANES, :].T


def kernel(
    parts, samples, planes,
    conc, classes, conductivity, wells, control,
    final_out, adjoint_out, gradient_out,
    cond, cond_t, xl, xu, xi, xe, xf, yl, yu, yi, ye, yf, zu, zi,
    field, held, field_t, held_t, later_t, source_t, final_t, adjoint_t,
    hits_x, hits_y, halo_send, halo, corner, joint_x, joint_y, ends, ps, qs,
    landed, part_sum, sample_sum, term_sum, sample_term,
    send_sem, recv_sem, bulk_send, bulk_recv, sample_send, sample_recv, halo_ssem, halo_rsem,
):
    me = lax.axis_index("space")
    own = lax.axis_index("sample")
    block = conc.shape[0] // planes
    grid_cells = conc.shape[1]
    length_t = grid_cells // SUBLANES
    wide = conc.shape[0]

    barrier = pltpu.get_barrier_semaphore()

    def peer(k):
        return {"space": lax.rem(me + k, parts)}

    def partner(k):
        return {"sample": lax.rem(own + k, samples)}

    for k in range(1, parts):
        pl.semaphore_signal(barrier, inc=1, device_id=peer(k), device_id_type=MESH)
    for k in range(1, samples):
        pl.semaphore_signal(barrier, inc=1, device_id=partner(k), device_id_type=MESH)

    def spread_out(ref, phase):
        copies = []
        for k in range(1, parts):
            copy = pltpu.make_async_remote_copy(
                src_ref=ref.at[me], dst_ref=ref.at[me],
                send_sem=send_sem.at[phase, k], recv_sem=recv_sem.at[phase, k],
                device_id=peer(k), device_id_type=MESH)
            copy.start()
            copies.append(copy)
        return copies

    def spread_samples(ref, phase):
        copies = []
        for k in range(1, samples):
            copy = pltpu.make_async_remote_copy(
                src_ref=ref.at[own], dst_ref=ref.at[own],
                send_sem=sample_send.at[phase, k], recv_sem=sample_recv.at[phase, k],
                device_id=partner(k), device_id_type=MESH)
            copy.start()
            copies.append(copy)
        return copies

    def send_blocks(ref, phase):
        copies = []
        for k in range(1, parts):
            to = lax.rem(me + k, parts)
            copy = pltpu.make_async_remote_copy(
                src_ref=ref.at[:, pl.ds(pl.multiple_of(to * block, block), block)],
                dst_ref=landed.at[phase, me],
                send_sem=bulk_send.at[phase, k], recv_sem=bulk_recv.at[phase, k],
                device_id=peer(k), device_id_type=MESH)
            copy.start()
            copies.append(copy)
        landed[phase, me] = ref[:, pl.ds(pl.multiple_of(me * block, block), block), :]
        return copies

    pending = []

    def arrive(copies):
        for copy in copies:
            copy.wait_recv()
        pending.extend(copies)

    def fill(t, _):
        at = pl.ds(pl.multiple_of(t * SUBLANES, SUBLANES), SUBLANES)
        labels = classes[at, :]
        values = jnp.full(labels.shape, conductivity[0], jnp.float32)
        for label in range(1, conductivity.shape[0]):
            values = jnp.where(labels == label, conductivity[label], values)
        put(cond, at, values)
        return 0

    lax.fori_loop(0, wide // SUBLANES, fill, 0)
    halo_send[0] = take(cond, rows_at(block - 1, planes, block))
    halo_send[1] = take(cond, rows_at(0, planes, block))
    pl.semaphore_wait(barrier, parts - 1 + samples - 1)
    halo_copies = []
    for side, k in ((0, 1), (1, parts - 1)):
        copy = pltpu.make_async_remote_copy(
            src_ref=halo_send.at[side], dst_ref=halo.at[side],
            send_sem=halo_ssem.at[side], recv_sem=halo_rsem.at[side],
            device_id=peer(k), device_id_type=MESH)
        copy.start()
        halo_copies.append(copy)

    def factor_depth(t, _):
        start = t * SUBLANES
        here = take(cond, pl.ds(pl.multiple_of(start, SUBLANES), SUBLANES))
        behind = jnp.zeros(here.shape, jnp.float32)
        u = behind
        for z in range(planes):
            if z < planes - 1:
                after = take(cond, pl.ds(pl.multiple_of((z + 1) * block + start, SUBLANES), SUBLANES))
                ahead = 2.0 * here * after / (here + after)
            else:
                after, ahead = here, jnp.zeros(here.shape, jnp.float32)
            r = 1.0 / (1.0 + spread_depth * (behind + ahead) + spread_depth * behind * u)
            u = -spread_depth * ahead * r
            at = pl.ds(pl.multiple_of(z * block + start, SUBLANES), SUBLANES)
            put(zi, at, r)
            put(zu, at, u)
            here, behind = after, ahead
        return 0

    lax.fori_loop(0, block // SUBLANES, factor_depth, 0)
    tile_transpose(cond, cond_t)

    x_row = lax.broadcasted_iota(jnp.int32, hits_x.shape, 0) % block + me * block
    hits_x[...] = jnp.where(x_row == wells[0:1, :], 1.0, 0.0)
    y_row = lax.broadcasted_iota(jnp.int32, hits_y.shape, 0)
    hits_y[...] = jnp.where(y_row == wells[1:2, :], 1.0, 0.0)
    across_last = (((1,), (1,)), ((), ()))
    source = lax.dot_general(
        hits_x[0:block, :] * control[...], hits_y[...], across_last,
        precision=EXACT, preferred_element_type=jnp.float32)
    for z in range(planes):
        cut = slice(z * block, (z + 1) * block)
        put(field, cut, conc[cut, :] + source)

    arrive(halo_copies)
    x_factors = (xl, xu, xi, xe, xf)
    not_first = (me > 0).astype(jnp.float32)
    not_last = (me < parts - 1).astype(jnp.float32)
    first_row = take(cond, rows_at(0, planes, block))
    face_before = not_first * 2.0 * halo[0] * first_row / (halo[0] + first_row)

    def beyond_x(first, last):
        return not_last * 2.0 * halo[1] * last / (halo[1] + last)

    corners = factor_blocks(
        cond, x_factors, planes, block, face_before, beyond_x, spread_along, drift_along)
    gff, glf, gfl, gll, face_ahead = corners
    for j, value in enumerate((gff, glf, gfl, gll, face_before, face_ahead)):
        corner[me, j * planes : (j + 1) * planes, :] = value
    corner_copies = spread_out(corner, 0)

    def ends_out(phase, first, last):
        ends[phase, me, 0:planes, :] = first
        ends[phase, me, planes : 2 * planes, :] = last
        copies = []
        for k in range(1, parts):
            copy = pltpu.make_async_remote_copy(
                src_ref=ends.at[phase, me], dst_ref=ends.at[phase, me],
                send_sem=send_sem.at[phase + 1, k], recv_sem=recv_sem.at[phase + 1, k],
                device_id=peer(k), device_id_type=MESH)
            copy.start()
            copies.append(copy)
        return copies

    def start_x(values, out, phase, flipped):
        low, weights = (xu, xe) if flipped else (xl, xf)
        first, last = sweep_down(values, out, low, xi, weights, planes, block)
        return ends_out(phase, first, last)

    def finish_x(copies, inner, out, phase, flipped):
        arrive(copies)
        way = 1 if flipped else 0
        joint = lambda b, j: joint_x[way, b, j * planes : (j + 1) * planes, :]
        firsts = [ends[phase, b, 0:planes, :] for b in range(parts)]
        alphas = []
        alpha = None
        for b in range(parts):
            last = ends[phase, b, planes : 2 * planes, :]
            alpha = last if b == 0 else last + joint(b, 0) * firsts[b] - joint(b, 1) * alpha
            alphas.append(alpha)
        zero = jnp.zeros_like(firsts[0])
        ps[parts] = zero
        qs[0] = zero
        p = zero
        for b in range(parts - 1, -1, -1):
            if b < parts - 1:
                qs[b + 1] = alphas[b] - joint(b, 5) * p
            value = joint(b, 2) * firsts[b] - joint(b, 4) * p
            if b > 0:
                value = value - joint(b, 3) * alphas[b - 1]
            p = value
            ps[b] = p
        coupling = -spread_along * face_before if flipped else -(spread_along * face_before + drift_along)
        incoming = coupling * qs[me]
        up, spike = (xl, xf) if flipped else (xu, xe)
        sweep_up(inner, out, up, spike, incoming, ps[me + 1], planes, block)

    x1 = start_x(field, held, 0, False)

    row = lax.broadcasted_iota(jnp.int32, (SUBLANES, wide), 0)
    y_factors = (yl, yu, yi, ye, yf)
    y_first = take(cond_t, rows_at(0, SUBLANES, length_t))
    y_last = take(cond_t, rows_at(length_t - 1, SUBLANES, length_t))
    last_before = pltpu.roll(y_last, 1, 0)
    y_before = jnp.where(row == 0, 0.0, 2.0 * last_before * y_first / (last_before + y_first))

    def beyond_y(first, last):
        after = pltpu.roll(first, SUBLANES - 1, 0)
        return jnp.where(row == SUBLANES - 1, 0.0, 2.0 * last * after / (last + after))

    gff, glf, gfl, gll, y_ahead = factor_blocks(
        cond_t, y_factors, SUBLANES, length_t, y_before, beyond_y, spread_across, drift_across)
    y_couplings = []
    for way in range(2):
        a = jnp.where(row == 0, 0.0, -(spread_across * y_before + drift_across))
        a_next = jnp.where(row == SUBLANES - 1, 0.0, -(spread_across * y_ahead + drift_across))
        c = -spread_across * y_before
        c_next = -spread_across * y_ahead
        if way == 0:
            vf, vl, wf, wl = a * gff, a * glf, c_next * gfl, c_next * gll
            y_couplings.append(a)
        else:
            vf, vl, wf, wl = c * gff, c * gfl, a_next * glf, a_next * gll
            y_couplings.append(c)
        beta = jnp.zeros((1, wide), jnp.float32)
        for b in range(SUBLANES):
            cut = slice(b, b + 1)
            terms = joint_terms(vf[cut], vl[cut], wf[cut], wl[cut], beta)
            beta = terms[5]
            for j, value in enumerate(terms):
                joint_y[way, j, b : b + 1, :] = value
        ahead = jnp.where(row == 0, 0.0, -joint_y[way, 1])
        back = -joint_y[way, 4]
        back = jnp.where(row == SUBLANES - 1, 0.0, back)
        for level, distance in enumerate((1, 2, 4)):
            joint_y[way, 6 + level] = ahead
            joint_y[way, 9 + level] = back
            ahead = jnp.where(row < 2 * distance, 0.0, ahead * pltpu.roll(ahead, distance, 0))
            back = jnp.where(
                row >= SUBLANES - 2 * distance, 0.0,
                back * pltpu.roll(back, SUBLANES - distance, 0))

    def solve_y(values, inner, out, flipped):
        way = 1 if flipped else 0
        low, weights = (yu, ye) if flipped else (yl, yf)
        up, spike = (yl, yf) if flipped else (yu, ye)
        first, last = sweep_down(values, inner, low, yi, weights, SUBLANES, length_t)
        alpha = last + joint_y[way, 0] * first
        for level, distance in enumerate((1, 2, 4)):
            alpha = alpha + joint_y[way, 6 + level] * pltpu.roll(alpha, distance, 0)
        alpha_before = jnp.where(row == 0, 0.0, pltpu.roll(alpha, 1, 0))
        p = joint_y[way, 2] * first - joint_y[way, 3] * alpha_before
        for level, distance in enumerate((1, 2, 4)):
            p = p + joint_y[way, 9 + level] * pltpu.roll(p, SUBLANES - distance, 0)
        p_next = jnp.where(row == SUBLANES - 1, 0.0, pltpu.roll(p, SUBLANES - 1, 0))
        q = alpha - joint_y[way, 5] * p_next
        q_before = jnp.where(row == 0, 0.0, pltpu.roll(q, 1, 0))
        incoming = y_couplings[way] * q_before
        sweep_up(inner, out, up, spike, incoming, p_next, SUBLANES, length_t)

    def solve_z(values):
        def body(t, _):
            start = t * SUBLANES
            ats = [pl.ds(pl.multiple_of(z * block + start, SUBLANES), SUBLANES) for z in range(planes)]
            ys = [take(values, ats[0])]
            us = [take(zu, at) for at in ats]
            for z in range(1, planes):
                ys.append(take(values, ats[z]) - us[z - 1] * ys[-1])
            x = ys[-1] * take(zi, ats[-1])
            put(values, ats[-1], x)
            for z in range(planes - 2, -1, -1):
                x = ys[z] * take(zi, ats[z]) - us[z] * x
                put(values, ats[z], x)
            return 0

        lax.fori_loop(0, block // SUBLANES, body, 0)

    put(source_t, slice(None), lax.dot_general(
        hits_y[...] * control[...], hits_x[...], across_last,
        precision=EXACT, preferred_element_type=jnp.float32))

    arrive(corner_copies)
    corner_of = lambda b, j: corner[b, j * planes : (j + 1) * planes, :]
    for way in range(2):
        beta = jnp.zeros((planes, grid_cells), jnp.float32)
        for b in range(parts):
            gff, glf, gfl, gll, behind, ahead = [corner_of(b, j) for j in range(6)]
            a = -(spread_along * behind + drift_along) if b > 0 else jnp.zeros_like(behind)
            a_next = -(spread_along * ahead + drift_along) if b < parts - 1 else jnp.zeros_like(ahead)
            c, c_next = -spread_along * behind, -spread_along * ahead
            if way == 0:
                terms = joint_terms(a * gff, a * glf, c_next * gfl, c_next * gll, beta)
            else:
                terms = joint_terms(c * gff, c * gfl, a_next * glf, a_next * gll, beta)
            beta = terms[5]
            for j, value in enumerate(terms):
                joint_x[way, b, j * planes : (j + 1) * planes, :] = value

    finish_x(x1, held, field, 0, False)
    solve_z(field)
    tile_transpose(field, field_t)
    solve_y(field_t, held_t, field_t, False)

    field_t[...] = field_t[...] + source_t[...]
    solve_y(field_t, held_t, field_t, False)
    tile_transpose(field_t, field)
    solve_z(field)
    x2 = start_x(field, held, 1, False)
    finish_x(x2, held, field, 1, False)

    x3 = start_x(field, held, 2, True)
    tile_transpose(field, final_t)
    final_copies = send_blocks(final_t, 0)

    def squares(t, total):
        value = take(field, pl.ds(pl.multiple_of(t * SUBLANES, SUBLANES), SUBLANES))
        return total + value * value

    total = lax.fori_loop(
        0, wide // SUBLANES, squares, jnp.zeros((SUBLANES, grid_cells), jnp.float32))
    part_sum[me] = 0.5 * sum(
        total[:, j : j + LANES] for j in range(0, grid_cells, LANES))
    misfit_copies = spread_out(part_sum, 5)

    finish_x(x3, held, field, 2, True)
    solve_z(field)
    tile_transpose(field, field_t)
    solve_y(field_t, held_t, later_t, True)
    arrive(misfit_copies)
    sample_sum[own] = sum(part_sum[b] for b in range(parts))
    sample_copies = spread_samples(sample_sum, 0)

    solve_y(later_t, held_t, field_t, True)
    tile_transpose(field_t, field)
    solve_z(field)
    x4 = start_x(field, held, 3, True)
    half = lax.broadcasted_iota(jnp.int32, (block, LANES), 1) < block

    def assemble(phase, out):
        for j in range(parts // 2):
            for w in range(planes // 2):
                left = landed[phase, 2 * j, w]
                right = landed[phase, 2 * j + 1, w]
                cut = slice(j * LANES, (j + 1) * LANES)
                out[2 * w, :, cut] = jnp.where(half, left, pltpu.roll(right, block, 1))
                out[2 * w + 1, :, cut] = jnp.where(half, pltpu.roll(left, block, 1), right)

    arrive(final_copies)
    assemble(0, final_out)
    finish_x(x4, held, field, 3, True)
    tile_transpose(field, adjoint_t)
    adjoint_copies = send_blocks(adjoint_t, 1)

    arrive(sample_copies)
    misfits = [jnp.sum(sample_sum[s], keepdims=True) for s in range(samples)]
    average = sum(misfits) / samples
    own_misfit = jnp.sum(sample_sum[own], keepdims=True)
    weight = (1.0 + aversion * (own_misfit - average) / (average + epsilon)) / samples
    picked = jnp.dot(
        take(later_t, slice(None)) + take(adjoint_t, slice(None)), hits_x[...],
        precision=EXACT, preferred_element_type=jnp.float32) * hits_y[...]
    picked = picked.reshape(grid_cells // SUBLANES, SUBLANES, picked.shape[1])
    term_sum[me] = weight * jnp.sum(picked, axis=0)
    term_copies = spread_out(term_sum, 6)
    arrive(term_copies)
    sample_term[own] = sum(term_sum[b] for b in range(parts))
    gradient_copies = spread_samples(sample_term, 1)
    arrive(gradient_copies)
    gradient_out[...] = jnp.sum(sum(sample_term[s] for s in range(samples)), axis=0, keepdims=True)

    arrive(adjoint_copies)
    assemble(1, adjoint_out)
    for copy in pending:
        copy.wait_send()


def fused(parts, samples, concentration, classes, conductivity, wells, control):
    _, planes, block, grid_cells = concentration.shape
    wide = planes * block
    count = wells.shape[1]
    f32 = jnp.float32
    vmem = lambda *shape: pltpu.VMEM(shape, f32)
    flat, turned = (grid_cells // LANES, wide, LANES), (wide // LANES, grid_cells, LANES)
    dma = pltpu.SemaphoreType.DMA
    scratch = [vmem(*flat), vmem(*turned)]
    scratch += [vmem(*flat)] * 5 + [vmem(*turned)] * 5 + [vmem(*flat)] * 2
    scratch += [vmem(*flat)] * 2 + [vmem(*turned)] * 6
    scratch += [
        vmem(wide, count), vmem(grid_cells, count),
        vmem(2, planes, grid_cells), vmem(2, planes, grid_cells),
        vmem(parts, 6 * planes, grid_cells),
        vmem(2, parts, 6 * planes, grid_cells),
        vmem(2, 12, SUBLANES, wide),
        vmem(4, parts, 2 * planes, grid_cells),
        vmem(parts + 1, planes, grid_cells), vmem(parts + 1, planes, grid_cells),
        vmem(2, parts, wide // LANES, block, LANES),
        vmem(parts, SUBLANES, LANES), vmem(samples, SUBLANES, LANES),
        vmem(parts, SUBLANES, count), vmem(samples, SUBLANES, count),
        dma((7, parts)), dma((7, parts)), dma((2, parts)), dma((2, parts)),
        dma((2, samples)), dma((2, samples)), dma((2,)), dma((2,)),
    ]
    on_vmem = pl.BlockSpec(memory_space=pltpu.VMEM)
    on_smem = pl.BlockSpec(memory_space=pltpu.SMEM)
    out = jax.ShapeDtypeStruct((planes, block, grid_cells), f32)
    final, adjoint, gradient = pl.pallas_call(
        functools.partial(kernel, parts, samples, planes),
        out_shape=(out, out, jax.ShapeDtypeStruct((1, count), f32)),
        in_specs=[on_vmem, on_vmem, on_smem, on_vmem, on_vmem],
        out_specs=(on_vmem, on_vmem, on_vmem),
        scratch_shapes=scratch,
        compiler_params=pltpu.CompilerParams(
            collective_id=0, has_side_effects=True, vmem_limit_bytes=48 * 1024 * 1024),
    )(
        concentration.reshape(wide, grid_cells), classes.reshape(wide, grid_cells), conductivity, wells,
        control.reshape(1, count))
    return final[None], adjoint[None], gradient.reshape(count)


def choose(axes, concentration, classes, conductivity, wells, control):
    parts, samples = axes["space"], axes["sample"]
    _, planes, block, grid_cells = concentration.shape
    fits = (
        2 * block == LANES and planes % 2 == 0 and parts % 2 == 0 and parts > 1
        and parts * block == grid_cells and grid_cells % LANES == 0
        and (planes * block) % LANES == 0
    )
    if fits:
        return fused(parts, samples, concentration, classes, conductivity, wells, control)
    return per_device(concentration, classes, conductivity, wells, control)


def solution(mesh):
    placed = (P("sample", None, "space", None), P("sample", None, "space", None), P(), P(), P())
    return jax.shard_map(
        functools.partial(choose, mesh.shape),
        mesh=mesh,
        in_specs=placed,
        out_specs=(P("sample", None, "space", None), P("sample", None, "space", None), P()),
        check_vma=False,
    )
```

```python
import functools
import jax
import jax.numpy as jnp
from jax import lax
from jax.experimental import pallas as pl
from jax.experimental.pallas import tpu as pltpu
from jax.sharding import PartitionSpec as P

spread_along = 200.0
drift_along = 6.0
spread_across = 200.0
drift_across = 3.0
spread_depth = 2.0
drift_depth = 0.0
aversion = 0.5
epsilon = 1e-06


def offset(values, amount, direction, filler):
    length = values.shape[direction]
    distance = abs(amount)
    margin = list(values.shape)
    margin[direction] = distance
    padding = jnp.full(margin, filler, values.dtype)
    if amount > 0:
        retained = lax.slice_in_dim(values, 0, length - distance, axis=direction)
        return jnp.concatenate([padding, retained], axis=direction)
    retained = lax.slice_in_dim(values, distance, length, axis=direction)
    return jnp.concatenate([retained, padding], axis=direction)


def line_terms(conduct, direction, spread, advection):
    following = offset(conduct, -1, direction, 0.0)
    face_ahead = 2.0 * conduct * following / (conduct + following)
    behind = offset(face_ahead, 1, direction, 0.0)
    subdiag = offset(-(spread * face_ahead + advection), 1, direction, 0.0)
    middle = 1.0 + spread * (behind + face_ahead) + advection
    superdiag = -spread * face_ahead
    return (subdiag, middle, superdiag)


def factor_lines(terms, direction):
    subdiag, middle, superdiag = terms
    length = middle.shape[direction]
    levels = []
    stride = 1
    while stride < length:
        middle_before = offset(middle, stride, direction, 1.0)
        middle_after = offset(middle, -stride, direction, 1.0)
        weight_below = -subdiag / middle_before
        weight_above = -superdiag / middle_after
        new_middle = (
            middle
            + weight_below * offset(superdiag, stride, direction, 0.0)
            + weight_above * offset(subdiag, -stride, direction, 0.0)
        )
        subdiag = weight_below * offset(subdiag, stride, direction, 0.0)
        superdiag = weight_above * offset(superdiag, -stride, direction, 0.0)
        middle = new_middle
        levels.append((weight_below, weight_above))
        stride = stride * 2
    return (levels, middle)


def solve_lines(values, factored, direction):
    levels, middle = factored
    stride = 1
    for weight_below, weight_above in levels:
        values = (
            values
            + weight_below * offset(values, stride, direction, 0.0)
            + weight_above * offset(values, -stride, direction, 0.0)
        )
        stride = stride * 2
    return values / middle


def solve_back(values, factored, direction):
    levels, middle = factored
    values = values / middle
    for depth_level in range(len(levels) - 1, -1, -1):
        weight_below, weight_above = levels[depth_level]
        stride = 2**depth_level
        values = (
            values
            + offset(weight_below * values, -stride, direction, 0.0)
            + offset(weight_above * values, stride, direction, 0.0)
        )
    return values


def pack_lines(values):
    planes, rows_here, length = values.shape
    count = lax.axis_size("space")
    return values.reshape(planes, rows_here, count, length // count).transpose(0, 2, 3, 1)


def unpack_lines(values):
    return values.reshape(values.shape[0], values.shape[2], values.shape[3])


def into_columns(values):
    return unpack_lines(
        lax.all_to_all(pack_lines(values), "space", split_axis=1, concat_axis=3, tiled=True)
    )


def into_rows(values):
    return unpack_lines(
        lax.all_to_all(pack_lines(values), "space", split_axis=1, concat_axis=3, tiled=True)
    )


def well_sum(column_sum, hits_rows, hits_columns):
    picked = jnp.dot(
        hits_rows, column_sum, precision=lax.Precision.HIGHEST, preferred_element_type=jnp.float32
    )
    return jnp.sum(picked * hits_columns, axis=1)


def per_device(concentration, classes, conductivity, wells, control):
    start_state = concentration[0]
    class_cells = classes[0]
    grid_cells = start_state.shape[2]
    block_size = start_state.shape[1]
    position = lax.axis_index("space")
    conduct_rows = jnp.zeros(class_cells.shape, jnp.float32)
    for class_label in range(conductivity.shape[0]):
        conduct_rows = conduct_rows + jnp.where(
            class_cells == class_label, conductivity[class_label], 0.0
        )
    conduct_columns = unpack_lines(
        lax.all_to_all(pack_lines(conduct_rows), "space", split_axis=1, concat_axis=3, tiled=True)
    )
    along_factor = factor_lines(line_terms(conduct_columns, 2, spread_along, drift_along), 2)
    across_factor = factor_lines(line_terms(conduct_rows, 2, spread_across, drift_across), 2)
    depth_rows = factor_lines(line_terms(conduct_rows, 0, spread_depth, drift_depth), 0)
    local_index = position * block_size + lax.iota(jnp.int32, block_size)
    all_index = lax.iota(jnp.int32, grid_cells)
    hits_first_local = (wells[0][:, None] == local_index[None, :]).astype(jnp.float32)
    hits_second_all = (wells[1][:, None] == all_index[None, :]).astype(jnp.float32)
    hits_second_local = (wells[1][:, None] == local_index[None, :]).astype(jnp.float32)
    hits_first_all = (wells[0][:, None] == all_index[None, :]).astype(jnp.float32)
    source = jnp.dot(
        hits_first_local.T,
        control[:, None] * hits_second_all,
        precision=lax.Precision.HIGHEST,
        preferred_element_type=jnp.float32,
    )
    depth_columns = factor_lines(line_terms(conduct_columns, 0, spread_depth, drift_depth), 0)
    current = into_columns(start_state + source[None])
    current = solve_lines(current, along_factor, 2)
    current = solve_lines(current, depth_columns, 0)
    current = into_rows(current)
    current = solve_lines(current, across_factor, 2)
    current = current + source[None]
    current = solve_lines(current, across_factor, 2)
    current = solve_lines(current, depth_rows, 0)
    final_state = solve_lines(into_columns(current), along_factor, 2)
    misfit_part = 0.5 * jnp.sum(final_state * final_state)
    second_adjoint = solve_back(final_state, along_factor, 2)
    second_adjoint = solve_back(second_adjoint, depth_columns, 0)
    second_adjoint = solve_back(into_rows(second_adjoint), across_factor, 2)
    first_adjoint = solve_back(second_adjoint, across_factor, 2)
    first_adjoint = solve_back(first_adjoint, depth_rows, 0)
    adjoint_state = solve_back(into_columns(first_adjoint), along_factor, 2)
    well_terms = well_sum(jnp.sum(second_adjoint, axis=0), hits_first_local, hits_second_all)
    well_terms = well_terms + well_sum(
        jnp.sum(adjoint_state, axis=0), hits_second_local, hits_first_all
    )
    sample_count = lax.axis_size("sample")
    own_misfit = lax.psum(misfit_part, "space")
    misfit_total = lax.psum(own_misfit, "sample")
    average = misfit_total / sample_count
    weight = (1.0 + aversion * (own_misfit - average) / (average + epsilon)) / sample_count
    gradient = lax.psum(weight * well_terms, ("sample", "space"))
    return (final_state[None], adjoint_state[None], gradient)


LANES = 128
SUBLANES = 8
UNROLL = 8
MESH = pl.DeviceIdType.MESH
EXACT = lax.Precision.HIGHEST


def steps(count, body, carry):
    def turn(t, state):
        for k in range(UNROLL):
            state = body(t * UNROLL + k, state)
        return state

    return lax.fori_loop(0, count // UNROLL, turn, carry)


def at_step(i):
    return pl.ds(pl.multiple_of(i * SUBLANES, SUBLANES), SUBLANES)


def gather_rows(ref, i, pieces, pitch):
    tiles = [ref[j, pl.ds(i, pieces, stride=pitch), :] for j in range(ref.shape[0])]
    groups = SUBLANES // pieces
    count = len(tiles) // groups
    tiles = [
        tiles[j] if groups == 1
        else jnp.concatenate([tiles[g * count + j] for g in range(groups)], axis=0)
        for j in range(count)
    ]
    return jnp.concatenate(tiles, axis=1)


def scatter_rows(ref, i, pieces, pitch, value):
    groups = SUBLANES // pieces
    count = ref.shape[0] // groups
    for j in range(ref.shape[0]):
        g, tile = j // count, j % count
        ref[j, pl.ds(i, pieces, stride=pitch), :] = value[
            g * pieces : (g + 1) * pieces, tile * LANES : (tile + 1) * LANES]


def take(ref, at):
    return jnp.concatenate([ref[j, at, :] for j in range(ref.shape[0])], axis=1)


def put(ref, at, value):
    for j in range(ref.shape[0]):
        ref[j, at, :] = value[:, j * LANES : (j + 1) * LANES]


def width(ref):
    return ref.shape[0] * LANES


def factor_blocks(read, factors, length, before, beyond, spread, drift):
    low, up, inv, from_first, to_first = factors
    shape = (SUBLANES, width(low))

    def body(i, state):
        here, behind, u, eta, eta_t, corner = state
        after = read(jnp.minimum(i + 1, length - 1))
        ahead = 2.0 * here * after / (here + after)
        ahead = jnp.where(i == length - 1, last_face, ahead)
        r = 1.0 / (1.0 + spread * (behind + ahead) + drift + (spread * behind + drift) * u)
        u = -spread * ahead * r
        lo = -(spread * ahead + drift) * r
        first = eta * r
        at = at_step(i)
        put(low, at, lo)
        put(up, at, u)
        put(inv, at, r)
        put(from_first, at, first)
        put(to_first, at, eta_t * r)
        return after, ahead, u, -lo * eta, -u * eta_t, corner + first * eta_t

    first_row = read(0)
    last_face = beyond(first_row, read(length - 1))
    ones = jnp.ones(shape, jnp.float32)
    zeros = jnp.zeros(shape, jnp.float32)
    state = steps(length, body, (first_row, before, zeros, ones, ones, zeros))
    at = at_step(length - 1)
    return state[5], take(from_first, at), take(to_first, at), take(inv, at), last_face


def sweep_down(read, out, low, inv, weights, length):
    def body(i, state):
        y, lo, total = state
        at = at_step(i)
        y = read(i) - lo * y
        put(out, at, y * take(inv, at))
        return y, take(low, at), total + take(weights, at) * y

    zeros = jnp.zeros((SUBLANES, width(low)), jnp.float32)
    _, _, total = steps(length, body, (zeros, zeros, zeros))
    return total, take(out, at_step(length - 1))


def sweep_up(held, write, up, spike, incoming, following, length):
    def body(k, x):
        i = length - 1 - k
        at = at_step(i)
        x = take(held, at) - take(spike, at) * incoming - take(up, at) * x
        write(i, x)
        return x

    steps(length, body, following)


def joint_terms(vf, vl, wf, wl, beta):
    r = 1.0 / (1.0 - vf * beta)
    s = vl * beta * r
    return s, vl + s * vf, r, r * vf, r * wf, wl + s * wf


def tile_transpose(source, target, length, pitch, pitch_to):
    for i in range(target.shape[0]):
        for j in range(source.shape[0]):
            tile = jnp.concatenate(
                [source[j, b * pitch : b * pitch + length, :] for b in (2 * i, 2 * i + 1)], axis=0).T
            for half in range(2):
                start = (2 * j + half) * pitch_to
                target[i, start : start + length, :] = tile[half * length : (half + 1) * length, :]


def kernel(
    parts, samples, planes,
    conc_in, classes_in, conductivity, wells, control,
    final_out, adjoint_out, gradient_out,
    conc, classes, in_sem, cond, cond_t, xl, xu, xi, xe, xf, yl, yu, yi, ye, yf, zu, zi,
    field, held, field_t, held_t, second_t, later_t, source_t, final_t, adjoint_t,
    hits_x, hits_y, hits_step, halo_send, halo, corner, joint_x, joint_y, ends, ps, qs,
    landed, part_sum, sample_sum, term_sum, sample_term,
    send_sem, recv_sem, bulk_send, bulk_recv, sample_send, sample_recv, halo_ssem, halo_rsem,
):
    me = lax.axis_index("space")
    own = lax.axis_index("sample")
    block = conc.shape[0] // planes
    grid_cells = conc.shape[1]
    length_t = grid_cells // SUBLANES
    wide = conc.shape[0]
    pitch, pitch_t = block + 1, length_t + 1
    class_copy = pltpu.make_async_copy(classes_in, classes, in_sem.at[0])
    class_copy.start()
    conc_copy = pltpu.make_async_copy(conc_in, conc, in_sem.at[1])
    conc_copy.start()

    barrier = pltpu.get_barrier_semaphore()

    def peer(k):
        return {"space": lax.rem(me + k, parts)}

    def partner(k):
        return {"sample": lax.rem(own + k, samples)}

    for k in range(1, parts):
        pl.semaphore_signal(barrier, inc=1, device_id=peer(k), device_id_type=MESH)
    for k in range(1, samples):
        pl.semaphore_signal(barrier, inc=1, device_id=partner(k), device_id_type=MESH)

    def spread_out(ref, phase):
        copies = []
        for k in range(1, parts):
            copy = pltpu.make_async_remote_copy(
                src_ref=ref.at[me], dst_ref=ref.at[me],
                send_sem=send_sem.at[phase, k], recv_sem=recv_sem.at[phase, k],
                device_id=peer(k), device_id_type=MESH)
            copy.start()
            copies.append(copy)
        return copies

    def spread_samples(ref, phase):
        copies = []
        for k in range(1, samples):
            copy = pltpu.make_async_remote_copy(
                src_ref=ref.at[own], dst_ref=ref.at[own],
                send_sem=sample_send.at[phase, k], recv_sem=sample_recv.at[phase, k],
                device_id=partner(k), device_id_type=MESH)
            copy.start()
            copies.append(copy)
        return copies

    def send_blocks(ref, phase):
        copies = []
        for k in range(1, parts):
            to = lax.rem(me + k, parts)
            copy = pltpu.make_async_remote_copy(
                src_ref=ref.at[:, pl.ds(pl.multiple_of(to * block, block), block)],
                dst_ref=landed.at[phase, me],
                send_sem=bulk_send.at[phase, k], recv_sem=bulk_recv.at[phase, k],
                device_id=peer(k), device_id_type=MESH)
            copy.start()
            copies.append(copy)
        landed[phase, me] = ref[:, pl.ds(pl.multiple_of(me * block, block), block), :]
        return copies

    pending = []

    def arrive(copies):
        for copy in copies:
            copy.wait_recv()
        pending.extend(copies)

    class_copy.wait()

    def x_rows(ref):
        return lambda i: gather_rows(ref, i, planes, pitch)

    def x_store(ref):
        return lambda i, value: scatter_rows(ref, i, planes, pitch, value)

    def y_rows(ref):
        return lambda i: gather_rows(ref, i, SUBLANES, pitch_t)

    def y_store(ref):
        return lambda i, value: scatter_rows(ref, i, SUBLANES, pitch_t, value)

    def in_order(ref):
        return lambda i: take(ref, at_step(i))

    for z in range(planes):
        for t in range(0, block, SUBLANES):
            labels = classes[z * block + t : z * block + t + SUBLANES, :]
            values = jnp.full(labels.shape, conductivity[0], jnp.float32)
            for label in range(1, conductivity.shape[0]):
                values = jnp.where(labels == label, conductivity[label], values)
            put(cond, slice(z * pitch + t, z * pitch + t + SUBLANES), values)
    x_cond = x_rows(cond)
    halo_send[0] = x_cond(block - 1)
    halo_send[1] = x_cond(0)
    pl.semaphore_wait(barrier, parts - 1 + samples - 1)
    halo_copies = []
    for side, k in ((0, 1), (1, parts - 1)):
        copy = pltpu.make_async_remote_copy(
            src_ref=halo_send.at[side], dst_ref=halo.at[side],
            send_sem=halo_ssem.at[side], recv_sem=halo_rsem.at[side],
            device_id=peer(k), device_id_type=MESH)
        copy.start()
        halo_copies.append(copy)

    for t in range(0, block, SUBLANES):
        here = take(cond, slice(t, t + SUBLANES))
        behind = jnp.zeros(here.shape, jnp.float32)
        u = behind
        for z in range(planes):
            if z < planes - 1:
                start = (z + 1) * pitch + t
                after = take(cond, slice(start, start + SUBLANES))
                ahead = 2.0 * here * after / (here + after)
            else:
                after, ahead = here, jnp.zeros(here.shape, jnp.float32)
            r = 1.0 / (1.0 + spread_depth * (behind + ahead) + spread_depth * behind * u)
            u = -spread_depth * ahead * r
            at = slice(z * block + t, z * block + t + SUBLANES)
            put(zi, at, r)
            put(zu, at, u)
            here, behind = after, ahead
    tile_transpose(cond, cond_t, block, pitch, pitch_t)

    x_row = lax.broadcasted_iota(jnp.int32, hits_x.shape, 0) % block + me * block
    hits_x[...] = jnp.where(x_row == wells[0:1, :], 1.0, 0.0)
    y_row = lax.broadcasted_iota(jnp.int32, hits_y.shape, 0)
    hits_y[...] = jnp.where(y_row == wells[1:2, :], 1.0, 0.0)
    y_row = y_row % SUBLANES * length_t + y_row // SUBLANES
    hits_step[...] = jnp.where(y_row == wells[1:2, :], 1.0, 0.0)
    across_last = (((1,), (1,)), ((), ()))
    source = lax.dot_general(
        hits_x[0:block, :] * control[...], hits_y[...], across_last,
        precision=EXACT, preferred_element_type=jnp.float32)
    conc_copy.wait()
    for z in range(planes):
        cut = slice(z * block, (z + 1) * block)
        put(field, slice(z * pitch, z * pitch + block), conc[cut, :] + source)

    arrive(halo_copies)
    x_factors = (xl, xu, xi, xe, xf)
    not_first = (me > 0).astype(jnp.float32)
    not_last = (me < parts - 1).astype(jnp.float32)
    first_row = x_cond(0)
    face_before = not_first * 2.0 * halo[0] * first_row / (halo[0] + first_row)

    def beyond_x(first, last):
        return not_last * 2.0 * halo[1] * last / (halo[1] + last)

    corners = factor_blocks(
        x_cond, x_factors, block, face_before, beyond_x, spread_along, drift_along)
    gff, glf, gfl, gll, face_ahead = corners
    for j, value in enumerate((gff, glf, gfl, gll, face_before, face_ahead)):
        corner[me, j * SUBLANES : (j + 1) * SUBLANES, :] = value
    corner_copies = spread_out(corner, 0)

    def ends_out(phase, first, last):
        ends[phase, me, 0:SUBLANES, :] = first
        ends[phase, me, SUBLANES : 2 * SUBLANES, :] = last
        copies = []
        for k in range(1, parts):
            copy = pltpu.make_async_remote_copy(
                src_ref=ends.at[phase, me], dst_ref=ends.at[phase, me],
                send_sem=send_sem.at[phase + 1, k], recv_sem=recv_sem.at[phase + 1, k],
                device_id=peer(k), device_id_type=MESH)
            copy.start()
            copies.append(copy)
        return copies

    def start_x(read, out, phase, flipped):
        low, weights = (xu, xe) if flipped else (xl, xf)
        first, last = sweep_down(read, out, low, xi, weights, block)
        return ends_out(phase, first, last)

    def finish_x(copies, inner, write, phase, flipped):
        arrive(copies)
        way = 1 if flipped else 0
        joint = lambda b, j: joint_x[way, b, j * SUBLANES : (j + 1) * SUBLANES, :]
        firsts = [ends[phase, b, 0:SUBLANES, :] for b in range(parts)]
        alphas = []
        alpha = None
        for b in range(parts):
            last = ends[phase, b, SUBLANES : 2 * SUBLANES, :]
            alpha = last if b == 0 else last + joint(b, 0) * firsts[b] - joint(b, 1) * alpha
            alphas.append(alpha)
        zero = jnp.zeros_like(firsts[0])
        ps[parts] = zero
        qs[0] = zero
        p = zero
        for b in range(parts - 1, -1, -1):
            if b < parts - 1:
                qs[b + 1] = alphas[b] - joint(b, 5) * p
            value = joint(b, 2) * firsts[b] - joint(b, 4) * p
            if b > 0:
                value = value - joint(b, 3) * alphas[b - 1]
            p = value
            ps[b] = p
        coupling = -spread_along * face_before if flipped else -(spread_along * face_before + drift_along)
        incoming = coupling * qs[me]
        up, spike = (xl, xf) if flipped else (xu, xe)
        sweep_up(inner, write, up, spike, incoming, ps[me + 1], block)

    x1 = start_x(x_rows(field), held, 0, False)

    row = lax.broadcasted_iota(jnp.int32, (SUBLANES, wide), 0)
    y_factors = (yl, yu, yi, ye, yf)
    y_cond = y_rows(cond_t)
    y_first = y_cond(0)
    y_last = y_cond(length_t - 1)
    last_before = pltpu.roll(y_last, 1, 0)
    y_before = jnp.where(row == 0, 0.0, 2.0 * last_before * y_first / (last_before + y_first))

    def beyond_y(first, last):
        after = pltpu.roll(first, SUBLANES - 1, 0)
        return jnp.where(row == SUBLANES - 1, 0.0, 2.0 * last * after / (last + after))

    gff, glf, gfl, gll, y_ahead = factor_blocks(
        y_cond, y_factors, length_t, y_before, beyond_y, spread_across, drift_across)
    y_couplings = []
    for way in range(2):
        a = jnp.where(row == 0, 0.0, -(spread_across * y_before + drift_across))
        a_next = jnp.where(row == SUBLANES - 1, 0.0, -(spread_across * y_ahead + drift_across))
        c = -spread_across * y_before
        c_next = -spread_across * y_ahead
        if way == 0:
            vf, vl, wf, wl = a * gff, a * glf, c_next * gfl, c_next * gll
            y_couplings.append(a)
        else:
            vf, vl, wf, wl = c * gff, c * gfl, a_next * glf, a_next * gll
            y_couplings.append(c)
        beta = jnp.zeros((1, wide), jnp.float32)
        for b in range(SUBLANES):
            cut = slice(b, b + 1)
            terms = joint_terms(vf[cut], vl[cut], wf[cut], wl[cut], beta)
            beta = terms[5]
            for j, value in enumerate(terms):
                joint_y[way, j, b : b + 1, :] = value
        ahead = jnp.where(row == 0, 0.0, -joint_y[way, 1])
        back = -joint_y[way, 4]
        back = jnp.where(row == SUBLANES - 1, 0.0, back)
        for level, distance in enumerate((1, 2, 4)):
            joint_y[way, 6 + level] = ahead
            joint_y[way, 9 + level] = back
            ahead = jnp.where(row < 2 * distance, 0.0, ahead * pltpu.roll(ahead, distance, 0))
            back = jnp.where(
                row >= SUBLANES - 2 * distance, 0.0,
                back * pltpu.roll(back, SUBLANES - distance, 0))

    def solve_y(read, inner, write, flipped):
        way = 1 if flipped else 0
        low, weights = (yu, ye) if flipped else (yl, yf)
        up, spike = (yl, yf) if flipped else (yu, ye)
        first, last = sweep_down(read, inner, low, yi, weights, length_t)
        alpha = last + joint_y[way, 0] * first
        for level, distance in enumerate((1, 2, 4)):
            alpha = alpha + joint_y[way, 6 + level] * pltpu.roll(alpha, distance, 0)
        alpha_before = jnp.where(row == 0, 0.0, pltpu.roll(alpha, 1, 0))
        p = joint_y[way, 2] * first - joint_y[way, 3] * alpha_before
        for level, distance in enumerate((1, 2, 4)):
            p = p + joint_y[way, 9 + level] * pltpu.roll(p, SUBLANES - distance, 0)
        p_next = jnp.where(row == SUBLANES - 1, 0.0, pltpu.roll(p, SUBLANES - 1, 0))
        q = alpha - joint_y[way, 5] * p_next
        q_before = jnp.where(row == 0, 0.0, pltpu.roll(q, 1, 0))
        incoming = y_couplings[way] * q_before
        sweep_up(inner, write, up, spike, incoming, p_next, length_t)

    def solve_z(values):
        for t in range(0, block, SUBLANES):
            ats = [slice(z * block + t, z * block + t + SUBLANES) for z in range(planes)]
            cells = [slice(z * pitch + t, z * pitch + t + SUBLANES) for z in range(planes)]
            ys = [take(values, cells[0])]
            us = [take(zu, at) for at in ats]
            for z in range(1, planes):
                ys.append(take(values, cells[z]) - us[z - 1] * ys[-1])
            x = ys[-1] * take(zi, ats[-1])
            put(values, cells[-1], x)
            for z in range(planes - 2, -1, -1):
                x = ys[z] * take(zi, ats[z]) - us[z] * x
                put(values, cells[z], x)

    source_turned = lax.dot_general(
        hits_y[...] * control[...], hits_x[...], across_last,
        precision=EXACT, preferred_element_type=jnp.float32)
    for b in range(SUBLANES):
        put(source_t, slice(b * pitch_t, b * pitch_t + length_t),
            source_turned[b * length_t : (b + 1) * length_t, :])

    arrive(corner_copies)
    corner_of = lambda b, j: corner[b, j * SUBLANES : (j + 1) * SUBLANES, :]
    for way in range(2):
        beta = jnp.zeros((SUBLANES, corner.shape[2]), jnp.float32)
        for b in range(parts):
            gff, glf, gfl, gll, behind, ahead = [corner_of(b, j) for j in range(6)]
            a = -(spread_along * behind + drift_along) if b > 0 else jnp.zeros_like(behind)
            a_next = -(spread_along * ahead + drift_along) if b < parts - 1 else jnp.zeros_like(ahead)
            c, c_next = -spread_along * behind, -spread_along * ahead
            if way == 0:
                terms = joint_terms(a * gff, a * glf, c_next * gfl, c_next * gll, beta)
            else:
                terms = joint_terms(c * gff, c * gfl, a_next * glf, a_next * gll, beta)
            beta = terms[5]
            for j, value in enumerate(terms):
                joint_x[way, b, j * SUBLANES : (j + 1) * SUBLANES, :] = value

    finish_x(x1, held, x_store(field), 0, False)
    solve_z(field)
    tile_transpose(field, field_t, block, pitch, pitch_t)
    with_source = lambda i, value: put(second_t, at_step(i), value + y_rows(source_t)(i))
    solve_y(y_rows(field_t), held_t, with_source, False)

    solve_y(in_order(second_t), held_t, y_store(field_t), False)
    tile_transpose(field_t, field, length_t, pitch_t, pitch)
    solve_z(field)
    x2 = start_x(x_rows(field), held, 1, False)
    finish_x(x2, held, x_store(field), 1, False)

    x3 = start_x(x_rows(field), held, 2, True)
    tile_transpose(field, final_t, block, pitch, length_t)
    final_copies = send_blocks(final_t, 0)

    total = jnp.zeros((SUBLANES, grid_cells), jnp.float32)
    for z in range(planes):
        for t in range(0, block, SUBLANES):
            value = take(field, slice(z * pitch + t, z * pitch + t + SUBLANES))
            total = total + value * value
    part_sum[me] = 0.5 * sum(
        total[:, j : j + LANES] for j in range(0, grid_cells, LANES))
    misfit_copies = spread_out(part_sum, 5)

    finish_x(x3, held, x_store(field), 2, True)
    solve_z(field)
    tile_transpose(field, field_t, block, pitch, pitch_t)
    solve_y(y_rows(field_t), held_t, lambda i, value: put(later_t, at_step(i), value), True)
    arrive(misfit_copies)
    sample_sum[own] = sum(part_sum[b] for b in range(parts))
    sample_copies = spread_samples(sample_sum, 0)

    solve_y(in_order(later_t), held_t, y_store(field_t), True)
    tile_transpose(field_t, field, length_t, pitch_t, pitch)
    solve_z(field)
    x4 = start_x(x_rows(field), held, 3, True)
    half = lax.broadcasted_iota(jnp.int32, (block, LANES), 1) < block

    def assemble(phase, out):
        for j in range(parts // 2):
            for w in range(planes // 2):
                left = landed[phase, 2 * j, w]
                right = landed[phase, 2 * j + 1, w]
                cut = slice(j * LANES, (j + 1) * LANES)
                out[2 * w, :, cut] = jnp.where(half, left, pltpu.roll(right, block, 1))
                out[2 * w + 1, :, cut] = jnp.where(half, pltpu.roll(left, block, 1), right)

    arrive(final_copies)
    assemble(0, final_out)
    finish_x(x4, held, x_store(field), 3, True)
    tile_transpose(field, adjoint_t, block, pitch, length_t)
    adjoint_copies = send_blocks(adjoint_t, 1)

    arrive(sample_copies)
    misfits = [jnp.sum(sample_sum[s], keepdims=True) for s in range(samples)]
    average = sum(misfits) / samples
    own_misfit = jnp.sum(sample_sum[own], keepdims=True)
    weight = (1.0 + aversion * (own_misfit - average) / (average + epsilon)) / samples
    picked = jnp.dot(
        take(adjoint_t, slice(None)), hits_x[...],
        precision=EXACT, preferred_element_type=jnp.float32) * hits_y[...]
    picked = picked + jnp.dot(
        take(later_t, slice(None)), hits_x[...],
        precision=EXACT, preferred_element_type=jnp.float32) * hits_step[...]
    picked = picked.reshape(grid_cells // SUBLANES, SUBLANES, picked.shape[1])
    term_sum[me] = weight * jnp.sum(picked, axis=0)
    term_copies = spread_out(term_sum, 6)
    arrive(term_copies)
    sample_term[own] = sum(term_sum[b] for b in range(parts))
    gradient_copies = spread_samples(sample_term, 1)
    arrive(gradient_copies)
    gradient_out[...] = jnp.sum(sum(sample_term[s] for s in range(samples)), axis=0, keepdims=True)

    arrive(adjoint_copies)
    assemble(1, adjoint_out)
    for copy in pending:
        copy.wait_send()


def fused(parts, samples, concentration, classes, conductivity, wells, control):
    _, planes, block, grid_cells = concentration.shape
    wide = planes * block
    count = wells.shape[1]
    f32 = jnp.float32
    vmem = lambda *shape: pltpu.VMEM(shape, f32)
    length_t = grid_cells // SUBLANES
    step = wide * grid_cells // block // SUBLANES
    flat = (grid_cells // LANES, planes * (block + 1), LANES)
    flat_even = (grid_cells // LANES, wide, LANES)
    turned = (wide // LANES, SUBLANES * (length_t + 1), LANES)
    turned_even = (wide // LANES, grid_cells, LANES)
    ordered = (step // LANES, block * SUBLANES, LANES)
    dma = pltpu.SemaphoreType.DMA
    scratch = [vmem(wide, grid_cells), pltpu.VMEM((wide, grid_cells), jnp.int32), dma((2,))]
    scratch += [vmem(*flat), vmem(*turned)]
    scratch += [vmem(*ordered)] * 5 + [vmem(*turned_even)] * 5 + [vmem(*flat_even)] * 2
    scratch += [vmem(*flat), vmem(*ordered), vmem(*turned), vmem(*turned_even)]
    scratch += [vmem(*turned_even)] * 2 + [vmem(*turned)] + [vmem(*turned_even)] * 2
    scratch += [
        vmem(wide, count), vmem(grid_cells, count), vmem(grid_cells, count),
        vmem(2, SUBLANES, step), vmem(2, SUBLANES, step),
        vmem(parts, 6 * SUBLANES, step),
        vmem(2, parts, 6 * SUBLANES, step),
        vmem(2, 12, SUBLANES, wide),
        vmem(4, parts, 2 * SUBLANES, step),
        vmem(parts + 1, SUBLANES, step), vmem(parts + 1, SUBLANES, step),
        vmem(2, parts, wide // LANES, block, LANES),
        vmem(parts, SUBLANES, LANES), vmem(samples, SUBLANES, LANES),
        vmem(parts, SUBLANES, count), vmem(samples, SUBLANES, count),
        dma((7, parts)), dma((7, parts)), dma((2, parts)), dma((2, parts)),
        dma((2, samples)), dma((2, samples)), dma((2,)), dma((2,)),
    ]
    on_vmem = pl.BlockSpec(memory_space=pltpu.VMEM)
    anywhere = pl.BlockSpec(memory_space=pl.ANY)
    on_smem = pl.BlockSpec(memory_space=pltpu.SMEM)
    out = jax.ShapeDtypeStruct((planes, block, grid_cells), f32)
    final, adjoint, gradient = pl.pallas_call(
        functools.partial(kernel, parts, samples, planes),
        out_shape=(out, out, jax.ShapeDtypeStruct((1, count), f32)),
        in_specs=[anywhere, anywhere, on_smem, on_vmem, on_vmem],
        out_specs=(on_vmem, on_vmem, on_vmem),
        scratch_shapes=scratch,
        compiler_params=pltpu.CompilerParams(
            collective_id=0, has_side_effects=True, vmem_limit_bytes=48 * 1024 * 1024),
    )(
        concentration.reshape(wide, grid_cells), classes.reshape(wide, grid_cells), conductivity, wells,
        control.reshape(1, count))
    return final[None], adjoint[None], gradient.reshape(count)


def choose(axes, concentration, classes, conductivity, wells, control):
    parts, samples = axes["space"], axes["sample"]
    _, planes, block, grid_cells = concentration.shape
    fits = (
        2 * block == LANES and planes % 2 == 0 and parts % 2 == 0 and parts > 1
        and parts * block == grid_cells and grid_cells % LANES == 0
        and (planes * block) % LANES == 0 and SUBLANES % planes == 0
        and (planes * grid_cells) % (SUBLANES * LANES) == 0 and grid_cells // SUBLANES == block
    )
    if fits:
        return fused(parts, samples, concentration, classes, conductivity, wells, control)
    return per_device(concentration, classes, conductivity, wells, control)


def solution(mesh):
    placed = (P("sample", None, "space", None), P("sample", None, "space", None), P(), P(), P())
    return jax.shard_map(
        functools.partial(choose, mesh.shape),
        mesh=mesh,
        in_specs=placed,
        out_specs=(P("sample", None, "space", None), P("sample", None, "space", None), P()),
        check_vma=False,
    )
```

```python
import functools
import jax
import jax.numpy as jnp
from jax import lax
from jax.experimental import pallas as pl
from jax.experimental.pallas import tpu as pltpu
from jax.sharding import PartitionSpec as P

spread_along = 200.0
drift_along = 6.0
spread_across = 200.0
drift_across = 3.0
spread_depth = 2.0
drift_depth = 0.0
aversion = 0.5
epsilon = 1e-06


def offset(values, amount, direction, filler):
    length = values.shape[direction]
    distance = abs(amount)
    margin = list(values.shape)
    margin[direction] = distance
    padding = jnp.full(margin, filler, values.dtype)
    if amount > 0:
        retained = lax.slice_in_dim(values, 0, length - distance, axis=direction)
        return jnp.concatenate([padding, retained], axis=direction)
    retained = lax.slice_in_dim(values, distance, length, axis=direction)
    return jnp.concatenate([retained, padding], axis=direction)


def line_terms(conduct, direction, spread, advection):
    following = offset(conduct, -1, direction, 0.0)
    face_ahead = 2.0 * conduct * following / (conduct + following)
    behind = offset(face_ahead, 1, direction, 0.0)
    subdiag = offset(-(spread * face_ahead + advection), 1, direction, 0.0)
    middle = 1.0 + spread * (behind + face_ahead) + advection
    superdiag = -spread * face_ahead
    return (subdiag, middle, superdiag)


def factor_lines(terms, direction):
    subdiag, middle, superdiag = terms
    length = middle.shape[direction]
    levels = []
    stride = 1
    while stride < length:
        middle_before = offset(middle, stride, direction, 1.0)
        middle_after = offset(middle, -stride, direction, 1.0)
        weight_below = -subdiag / middle_before
        weight_above = -superdiag / middle_after
        new_middle = (
            middle
            + weight_below * offset(superdiag, stride, direction, 0.0)
            + weight_above * offset(subdiag, -stride, direction, 0.0)
        )
        subdiag = weight_below * offset(subdiag, stride, direction, 0.0)
        superdiag = weight_above * offset(superdiag, -stride, direction, 0.0)
        middle = new_middle
        levels.append((weight_below, weight_above))
        stride = stride * 2
    return (levels, middle)


def solve_lines(values, factored, direction):
    levels, middle = factored
    stride = 1
    for weight_below, weight_above in levels:
        values = (
            values
            + weight_below * offset(values, stride, direction, 0.0)
            + weight_above * offset(values, -stride, direction, 0.0)
        )
        stride = stride * 2
    return values / middle


def solve_back(values, factored, direction):
    levels, middle = factored
    values = values / middle
    for depth_level in range(len(levels) - 1, -1, -1):
        weight_below, weight_above = levels[depth_level]
        stride = 2**depth_level
        values = (
            values
            + offset(weight_below * values, -stride, direction, 0.0)
            + offset(weight_above * values, stride, direction, 0.0)
        )
    return values


def pack_lines(values):
    planes, rows_here, length = values.shape
    count = lax.axis_size("space")
    return values.reshape(planes, rows_here, count, length // count).transpose(0, 2, 3, 1)


def unpack_lines(values):
    return values.reshape(values.shape[0], values.shape[2], values.shape[3])


def into_columns(values):
    return unpack_lines(
        lax.all_to_all(pack_lines(values), "space", split_axis=1, concat_axis=3, tiled=True)
    )


def into_rows(values):
    return unpack_lines(
        lax.all_to_all(pack_lines(values), "space", split_axis=1, concat_axis=3, tiled=True)
    )


def well_sum(column_sum, hits_rows, hits_columns):
    picked = jnp.dot(
        hits_rows, column_sum, precision=lax.Precision.HIGHEST, preferred_element_type=jnp.float32
    )
    return jnp.sum(picked * hits_columns, axis=1)


def per_device(concentration, classes, conductivity, wells, control):
    start_state = concentration[0]
    class_cells = classes[0]
    grid_cells = start_state.shape[2]
    block_size = start_state.shape[1]
    position = lax.axis_index("space")
    conduct_rows = jnp.zeros(class_cells.shape, jnp.float32)
    for class_label in range(conductivity.shape[0]):
        conduct_rows = conduct_rows + jnp.where(
            class_cells == class_label, conductivity[class_label], 0.0
        )
    conduct_columns = unpack_lines(
        lax.all_to_all(pack_lines(conduct_rows), "space", split_axis=1, concat_axis=3, tiled=True)
    )
    along_factor = factor_lines(line_terms(conduct_columns, 2, spread_along, drift_along), 2)
    across_factor = factor_lines(line_terms(conduct_rows, 2, spread_across, drift_across), 2)
    depth_rows = factor_lines(line_terms(conduct_rows, 0, spread_depth, drift_depth), 0)
    local_index = position * block_size + lax.iota(jnp.int32, block_size)
    all_index = lax.iota(jnp.int32, grid_cells)
    hits_first_local = (wells[0][:, None] == local_index[None, :]).astype(jnp.float32)
    hits_second_all = (wells[1][:, None] == all_index[None, :]).astype(jnp.float32)
    hits_second_local = (wells[1][:, None] == local_index[None, :]).astype(jnp.float32)
    hits_first_all = (wells[0][:, None] == all_index[None, :]).astype(jnp.float32)
    source = jnp.dot(
        hits_first_local.T,
        control[:, None] * hits_second_all,
        precision=lax.Precision.HIGHEST,
        preferred_element_type=jnp.float32,
    )
    depth_columns = factor_lines(line_terms(conduct_columns, 0, spread_depth, drift_depth), 0)
    current = into_columns(start_state + source[None])
    current = solve_lines(current, along_factor, 2)
    current = solve_lines(current, depth_columns, 0)
    current = into_rows(current)
    current = solve_lines(current, across_factor, 2)
    current = current + source[None]
    current = solve_lines(current, across_factor, 2)
    current = solve_lines(current, depth_rows, 0)
    final_state = solve_lines(into_columns(current), along_factor, 2)
    misfit_part = 0.5 * jnp.sum(final_state * final_state)
    second_adjoint = solve_back(final_state, along_factor, 2)
    second_adjoint = solve_back(second_adjoint, depth_columns, 0)
    second_adjoint = solve_back(into_rows(second_adjoint), across_factor, 2)
    first_adjoint = solve_back(second_adjoint, across_factor, 2)
    first_adjoint = solve_back(first_adjoint, depth_rows, 0)
    adjoint_state = solve_back(into_columns(first_adjoint), along_factor, 2)
    well_terms = well_sum(jnp.sum(second_adjoint, axis=0), hits_first_local, hits_second_all)
    well_terms = well_terms + well_sum(
        jnp.sum(adjoint_state, axis=0), hits_second_local, hits_first_all
    )
    sample_count = lax.axis_size("sample")
    own_misfit = lax.psum(misfit_part, "space")
    misfit_total = lax.psum(own_misfit, "sample")
    average = misfit_total / sample_count
    weight = (1.0 + aversion * (own_misfit - average) / (average + epsilon)) / sample_count
    gradient = lax.psum(weight * well_terms, ("sample", "space"))
    return (final_state[None], adjoint_state[None], gradient)


LANES = 128
SUBLANES = 8
UNROLL = 8
MESH = pl.DeviceIdType.MESH
EXACT = lax.Precision.HIGHEST


def steps(count, load, work, store, carry):
    def turn(t, state):
        group = [t * UNROLL + k for k in range(UNROLL)]
        loaded = [load(i) for i in group]
        results = []
        for i, values in zip(group, loaded):
            state, result = work(i, state, values)
            results.append(result)
        for i, result in zip(group, results):
            store(i, result)
        return state

    return lax.fori_loop(0, count // UNROLL, turn, carry)


def at_step(i):
    return pl.ds(pl.multiple_of(i * SUBLANES, SUBLANES), SUBLANES)


def gather_rows(ref, i, pitch):
    return take(ref, pl.ds(i, SUBLANES, stride=pitch))


def scatter_rows(ref, i, pitch, value):
    put(ref, pl.ds(i, SUBLANES, stride=pitch), value)


def take(ref, at):
    return jnp.concatenate([ref[j, at, :] for j in range(ref.shape[0])], axis=1)


def put(ref, at, value):
    for j in range(ref.shape[0]):
        ref[j, at, :] = value[:, j * LANES : (j + 1) * LANES]


def width(ref):
    return ref.shape[0] * LANES


def factor_blocks(lines, length):
    def load(i):
        return [line[0](jnp.minimum(i + 1, length - 1)) for line in lines]

    def work(i, states, loaded):
        new_states, results = [], []
        for (_, _, _, last_face, spread, drift), state, after in zip(lines, states, loaded):
            here, behind, u, eta, eta_t, corner = state
            ahead = 2.0 * here * after / (here + after)
            ahead = jnp.where(i == length - 1, last_face, ahead)
            r = 1.0 / (1.0 + spread * (behind + ahead) + drift + (spread * behind + drift) * u)
            u = -spread * ahead * r
            lo = -(spread * ahead + drift) * r
            first = eta * r
            new_states.append((after, ahead, u, -lo * eta, -u * eta_t, corner + first * eta_t))
            results.append((lo, u, r, first, eta_t * r))
        return new_states, results

    def store(i, results):
        for line, result in zip(lines, results):
            for ref, value in zip(line[1], result):
                put(ref, at_step(i), value)

    start = []
    for read, factors, before, _, _, _ in lines:
        ones = jnp.ones((SUBLANES, width(factors[0])), jnp.float32)
        zeros = jnp.zeros_like(ones)
        start.append((read(0), before, zeros, ones, ones, zeros))
    states = steps(length, load, work, store, start)
    at = at_step(length - 1)
    corners = []
    for line, state in zip(lines, states):
        _, _, inv, from_first, to_first = line[1]
        corners.append((state[5], take(from_first, at), take(to_first, at), take(inv, at)))
    return corners


def sweep_down(read, out, low, inv, weights, length):
    def load(i):
        at = at_step(i)
        return read(i), take(inv, at), take(low, at), take(weights, at)

    def work(i, state, values):
        y, lo, total = state
        here, r, lo_next, share = values
        y = here - lo * y
        return (y, lo_next, total + share * y), y * r

    def store(i, z):
        put(out, at_step(i), z)

    zeros = jnp.zeros((SUBLANES, width(low)), jnp.float32)
    _, _, total = steps(length, load, work, store, (zeros, zeros, zeros))
    return total, take(out, at_step(length - 1))


def sweep_up(held, write, up, spike, incoming, following, length):
    def load(k):
        at = at_step(length - 1 - k)
        return take(held, at), take(spike, at), take(up, at)

    def work(k, x, values):
        here, share, factor = values
        x = here - share * incoming - factor * x
        return x, x

    def store(k, x):
        write(length - 1 - k, x)

    steps(length, load, work, store, following)


def joint_terms(vf, vl, wf, wl, beta):
    r = 1.0 / (1.0 - vf * beta)
    s = vl * beta * r
    return s, vl + s * vf, r, r * vf, r * wf, wl + s * wf


def turn_over(source, target, planes, length, pitch, pitch_to):
    tiles = source.shape[0]
    for i in range(target.shape[0]):
        for j in range(target.shape[1] // pitch_to // 2):
            first = j // tiles * planes + 2 * i
            tile = jnp.concatenate(
                [source[j % tiles, b * pitch : b * pitch + length, :] for b in (first, first + 1)],
                axis=0).T
            for half in range(2):
                start = (2 * j + half) * pitch_to
                target[i, start : start + length, :] = tile[half * length : (half + 1) * length, :]


def turn_back(source, target, planes, length, pitch, pitch_to):
    tiles = target.shape[0]
    for i in range(source.shape[0]):
        for j in range(source.shape[1] // pitch // 2):
            tile = jnp.concatenate(
                [source[i, b * pitch : b * pitch + length, :] for b in (2 * j, 2 * j + 1)], axis=0).T
            for half in range(2):
                start = (j // tiles * planes + 2 * i + half) * pitch_to
                target[j % tiles, start : start + length, :] = tile[
                    half * length : (half + 1) * length, :]


def kernel(
    parts, samples, planes,
    conc_in, classes_in, conductivity, wells, control,
    final_out, adjoint_out, gradient_out,
    conc, classes, in_sem, cond, cond_t, xl, xu, xi, xe, xf, yl, yu, yi, ye, yf, zu, zi,
    field, held, field_t, held_t, second_t, later_t, source_t, final_t, adjoint_t,
    hits_x, hits_y, hits_step, halo_send, halo, corner, joint_x, joint_y, ends, ps, qs,
    landed, part_sum, sample_sum, term_sum, sample_term,
    send_sem, recv_sem, bulk_send, bulk_recv, sample_send, sample_recv, halo_ssem, halo_rsem,
):
    me = lax.axis_index("space")
    own = lax.axis_index("sample")
    block = conc.shape[0] // planes
    grid_cells = conc.shape[1]
    length_t = grid_cells // SUBLANES
    wide = conc.shape[0]
    pitch, pitch_t = block + 1, length_t + 1
    class_copy = pltpu.make_async_copy(classes_in, classes, in_sem.at[0])
    class_copy.start()
    conc_copy = pltpu.make_async_copy(conc_in, conc, in_sem.at[1])
    conc_copy.start()

    barrier = pltpu.get_barrier_semaphore()

    def peer(k):
        return {"space": lax.rem(me + k, parts)}

    def partner(k):
        return {"sample": lax.rem(own + k, samples)}

    for k in range(1, parts):
        pl.semaphore_signal(barrier, inc=1, device_id=peer(k), device_id_type=MESH)
    for k in range(1, samples):
        pl.semaphore_signal(barrier, inc=1, device_id=partner(k), device_id_type=MESH)

    def spread_out(ref, phase):
        copies = []
        for k in range(1, parts):
            copy = pltpu.make_async_remote_copy(
                src_ref=ref.at[me], dst_ref=ref.at[me],
                send_sem=send_sem.at[phase, k], recv_sem=recv_sem.at[phase, k],
                device_id=peer(k), device_id_type=MESH)
            copy.start()
            copies.append(copy)
        return copies

    def spread_samples(ref, phase):
        copies = []
        for k in range(1, samples):
            copy = pltpu.make_async_remote_copy(
                src_ref=ref.at[own], dst_ref=ref.at[own],
                send_sem=sample_send.at[phase, k], recv_sem=sample_recv.at[phase, k],
                device_id=partner(k), device_id_type=MESH)
            copy.start()
            copies.append(copy)
        return copies

    def send_blocks(ref, phase):
        copies = []
        for k in range(1, parts):
            to = lax.rem(me + k, parts)
            copy = pltpu.make_async_remote_copy(
                src_ref=ref.at[:, pl.ds(pl.multiple_of(to * block, block), block)],
                dst_ref=landed.at[phase, me],
                send_sem=bulk_send.at[phase, k], recv_sem=bulk_recv.at[phase, k],
                device_id=peer(k), device_id_type=MESH)
            copy.start()
            copies.append(copy)
        landed[phase, me] = ref[:, pl.ds(pl.multiple_of(me * block, block), block), :]
        return copies

    pending = []

    def arrive(copies):
        for copy in copies:
            copy.wait_recv()
        pending.extend(copies)

    class_copy.wait()

    def x_rows(ref):
        return lambda i: gather_rows(ref, i, pitch)

    def x_store(ref):
        return lambda i, value: scatter_rows(ref, i, pitch, value)

    def y_rows(ref):
        return lambda i: gather_rows(ref, i, pitch_t)

    def y_store(ref):
        return lambda i, value: scatter_rows(ref, i, pitch_t, value)

    def in_order(ref):
        return lambda i: take(ref, at_step(i))

    groups = SUBLANES // planes
    columns = grid_cells // groups
    for g in range(groups):
        for z in range(planes):
            for t in range(0, block, SUBLANES):
                start = z * block + t
                labels = classes[start : start + SUBLANES, g * columns : (g + 1) * columns]
                values = jnp.full(labels.shape, conductivity[0], jnp.float32)
                for label in range(1, conductivity.shape[0]):
                    values = jnp.where(labels == label, conductivity[label], values)
                start = (g * planes + z) * pitch + t
                put(cond, slice(start, start + SUBLANES), values)
    x_cond = x_rows(cond)
    halo_send[0] = x_cond(block - 1)
    halo_send[1] = x_cond(0)
    pl.semaphore_wait(barrier, parts - 1 + samples - 1)
    halo_copies = []
    for side, k in ((0, 1), (1, parts - 1)):
        copy = pltpu.make_async_remote_copy(
            src_ref=halo_send.at[side], dst_ref=halo.at[side],
            send_sem=halo_ssem.at[side], recv_sem=halo_rsem.at[side],
            device_id=peer(k), device_id_type=MESH)
        copy.start()
        halo_copies.append(copy)

    for g, t in [(g, t) for g in range(groups) for t in range(0, block, SUBLANES)]:
        start = g * planes * pitch + t
        here = take(cond, slice(start, start + SUBLANES))
        behind = jnp.zeros(here.shape, jnp.float32)
        u = behind
        for z in range(planes):
            if z < planes - 1:
                start = (g * planes + z + 1) * pitch + t
                after = take(cond, slice(start, start + SUBLANES))
                ahead = 2.0 * here * after / (here + after)
            else:
                after, ahead = here, jnp.zeros(here.shape, jnp.float32)
            r = 1.0 / (1.0 + spread_depth * (behind + ahead) + spread_depth * behind * u)
            u = -spread_depth * ahead * r
            start = (g * planes + z) * block + t
            put(zi, slice(start, start + SUBLANES), r)
            put(zu, slice(start, start + SUBLANES), u)
            here, behind = after, ahead
    turn_over(cond, cond_t, planes, block, pitch, pitch_t)

    x_row = lax.broadcasted_iota(jnp.int32, hits_x.shape, 0) % block + me * block
    hits_x[...] = jnp.where(x_row == wells[0:1, :], 1.0, 0.0)
    y_row = lax.broadcasted_iota(jnp.int32, hits_y.shape, 0)
    hits_y[...] = jnp.where(y_row == wells[1:2, :], 1.0, 0.0)
    y_row = y_row % SUBLANES * length_t + y_row // SUBLANES
    hits_step[...] = jnp.where(y_row == wells[1:2, :], 1.0, 0.0)
    across_last = (((1,), (1,)), ((), ()))
    source = lax.dot_general(
        hits_x[0:block, :] * control[...], hits_y[...], across_last,
        precision=EXACT, preferred_element_type=jnp.float32)
    conc_copy.wait()
    for g in range(groups):
        cut = slice(g * columns, (g + 1) * columns)
        for z in range(planes):
            start = (g * planes + z) * pitch
            put(field, slice(start, start + block),
                conc[z * block : (z + 1) * block, cut] + source[:, cut])

    row = lax.broadcasted_iota(jnp.int32, (SUBLANES, wide), 0)
    y_factors = (yl, yu, yi, ye, yf)
    y_cond = y_rows(cond_t)
    y_first = y_cond(0)
    y_last = y_cond(length_t - 1)
    last_before = pltpu.roll(y_last, 1, 0)
    y_before = jnp.where(row == 0, 0.0, 2.0 * last_before * y_first / (last_before + y_first))

    first_after = pltpu.roll(y_first, SUBLANES - 1, 0)
    y_ahead = jnp.where(row == SUBLANES - 1, 0.0, 2.0 * y_last * first_after / (y_last + first_after))

    arrive(halo_copies)
    x_factors = (xl, xu, xi, xe, xf)
    not_first = (me > 0).astype(jnp.float32)
    not_last = (me < parts - 1).astype(jnp.float32)
    first_row = x_cond(0)
    face_before = not_first * 2.0 * halo[0] * first_row / (halo[0] + first_row)

    last_row = x_cond(block - 1)
    face_ahead = not_last * 2.0 * halo[1] * last_row / (halo[1] + last_row)
    (gff, glf, gfl, gll), y_corners = factor_blocks(
        (
            (x_cond, x_factors, face_before, face_ahead, spread_along, drift_along),
            (y_cond, y_factors, y_before, y_ahead, spread_across, drift_across),
        ), block)
    for j, value in enumerate((gff, glf, gfl, gll, face_before, face_ahead)):
        corner[me, j * SUBLANES : (j + 1) * SUBLANES, :] = value
    corner_copies = spread_out(corner, 0)

    def ends_out(phase, first, last):
        ends[phase, me, 0:SUBLANES, :] = first
        ends[phase, me, SUBLANES : 2 * SUBLANES, :] = last
        copies = []
        for k in range(1, parts):
            copy = pltpu.make_async_remote_copy(
                src_ref=ends.at[phase, me], dst_ref=ends.at[phase, me],
                send_sem=send_sem.at[phase + 1, k], recv_sem=recv_sem.at[phase + 1, k],
                device_id=peer(k), device_id_type=MESH)
            copy.start()
            copies.append(copy)
        return copies

    def start_x(read, out, phase, flipped):
        low, weights = (xu, xe) if flipped else (xl, xf)
        first, last = sweep_down(read, out, low, xi, weights, block)
        return ends_out(phase, first, last)

    def finish_x(copies, inner, write, phase, flipped):
        arrive(copies)
        way = 1 if flipped else 0
        joint = lambda b, j: joint_x[way, b, j * SUBLANES : (j + 1) * SUBLANES, :]
        firsts = [ends[phase, b, 0:SUBLANES, :] for b in range(parts)]
        alphas = []
        alpha = None
        for b in range(parts):
            last = ends[phase, b, SUBLANES : 2 * SUBLANES, :]
            alpha = last if b == 0 else last + joint(b, 0) * firsts[b] - joint(b, 1) * alpha
            alphas.append(alpha)
        zero = jnp.zeros_like(firsts[0])
        ps[parts] = zero
        qs[0] = zero
        p = zero
        for b in range(parts - 1, -1, -1):
            if b < parts - 1:
                qs[b + 1] = alphas[b] - joint(b, 5) * p
            value = joint(b, 2) * firsts[b] - joint(b, 4) * p
            if b > 0:
                value = value - joint(b, 3) * alphas[b - 1]
            p = value
            ps[b] = p
        coupling = -spread_along * face_before if flipped else -(spread_along * face_before + drift_along)
        incoming = coupling * qs[me]
        up, spike = (xl, xf) if flipped else (xu, xe)
        sweep_up(inner, write, up, spike, incoming, ps[me + 1], block)

    x1 = start_x(x_rows(field), held, 0, False)

    gff, glf, gfl, gll = y_corners
    y_couplings = []
    for way in range(2):
        a = jnp.where(row == 0, 0.0, -(spread_across * y_before + drift_across))
        a_next = jnp.where(row == SUBLANES - 1, 0.0, -(spread_across * y_ahead + drift_across))
        c = -spread_across * y_before
        c_next = -spread_across * y_ahead
        if way == 0:
            vf, vl, wf, wl = a * gff, a * glf, c_next * gfl, c_next * gll
            y_couplings.append(a)
        else:
            vf, vl, wf, wl = c * gff, c * gfl, a_next * glf, a_next * gll
            y_couplings.append(c)
        beta = jnp.zeros((1, wide), jnp.float32)
        for b in range(SUBLANES):
            cut = slice(b, b + 1)
            terms = joint_terms(vf[cut], vl[cut], wf[cut], wl[cut], beta)
            beta = terms[5]
            for j, value in enumerate(terms):
                joint_y[way, j, b : b + 1, :] = value
        ahead = jnp.where(row == 0, 0.0, -joint_y[way, 1])
        back = -joint_y[way, 4]
        back = jnp.where(row == SUBLANES - 1, 0.0, back)
        for level, distance in enumerate((1, 2, 4)):
            joint_y[way, 6 + level] = ahead
            joint_y[way, 9 + level] = back
            ahead = jnp.where(row < 2 * distance, 0.0, ahead * pltpu.roll(ahead, distance, 0))
            back = jnp.where(
                row >= SUBLANES - 2 * distance, 0.0,
                back * pltpu.roll(back, SUBLANES - distance, 0))

    def solve_y(read, inner, write, flipped):
        way = 1 if flipped else 0
        low, weights = (yu, ye) if flipped else (yl, yf)
        up, spike = (yl, yf) if flipped else (yu, ye)
        first, last = sweep_down(read, inner, low, yi, weights, length_t)
        alpha = last + joint_y[way, 0] * first
        for level, distance in enumerate((1, 2, 4)):
            alpha = alpha + joint_y[way, 6 + level] * pltpu.roll(alpha, distance, 0)
        alpha_before = jnp.where(row == 0, 0.0, pltpu.roll(alpha, 1, 0))
        p = joint_y[way, 2] * first - joint_y[way, 3] * alpha_before
        for level, distance in enumerate((1, 2, 4)):
            p = p + joint_y[way, 9 + level] * pltpu.roll(p, SUBLANES - distance, 0)
        p_next = jnp.where(row == SUBLANES - 1, 0.0, pltpu.roll(p, SUBLANES - 1, 0))
        q = alpha - joint_y[way, 5] * p_next
        q_before = jnp.where(row == 0, 0.0, pltpu.roll(q, 1, 0))
        incoming = y_couplings[way] * q_before
        sweep_up(inner, write, up, spike, incoming, p_next, length_t)

    def solve_z(values):
        for g, t in [(g, t) for g in range(groups) for t in range(0, block, SUBLANES)]:
            ats = [(g * planes + z) * block + t for z in range(planes)]
            cells = [(g * planes + z) * pitch + t for z in range(planes)]
            ats = [slice(start, start + SUBLANES) for start in ats]
            cells = [slice(start, start + SUBLANES) for start in cells]
            ys = [take(values, cells[0])]
            us = [take(zu, at) for at in ats]
            for z in range(1, planes):
                ys.append(take(values, cells[z]) - us[z - 1] * ys[-1])
            x = ys[-1] * take(zi, ats[-1])
            put(values, cells[-1], x)
            for z in range(planes - 2, -1, -1):
                x = ys[z] * take(zi, ats[z]) - us[z] * x
                put(values, cells[z], x)

    source_turned = lax.dot_general(
        hits_y[...] * control[...], hits_x[...], across_last,
        precision=EXACT, preferred_element_type=jnp.float32)
    for b in range(SUBLANES):
        put(source_t, slice(b * pitch_t, b * pitch_t + length_t),
            source_turned[b * length_t : (b + 1) * length_t, :])

    arrive(corner_copies)
    corner_of = lambda b, j: corner[b, j * SUBLANES : (j + 1) * SUBLANES, :]
    for way in range(2):
        beta = jnp.zeros((SUBLANES, corner.shape[2]), jnp.float32)
        for b in range(parts):
            gff, glf, gfl, gll, behind, ahead = [corner_of(b, j) for j in range(6)]
            a = -(spread_along * behind + drift_along) if b > 0 else jnp.zeros_like(behind)
            a_next = -(spread_along * ahead + drift_along) if b < parts - 1 else jnp.zeros_like(ahead)
            c, c_next = -spread_along * behind, -spread_along * ahead
            if way == 0:
                terms = joint_terms(a * gff, a * glf, c_next * gfl, c_next * gll, beta)
            else:
                terms = joint_terms(c * gff, c * gfl, a_next * glf, a_next * gll, beta)
            beta = terms[5]
            for j, value in enumerate(terms):
                joint_x[way, b, j * SUBLANES : (j + 1) * SUBLANES, :] = value

    finish_x(x1, held, x_store(field), 0, False)
    solve_z(field)
    turn_over(field, field_t, planes, block, pitch, pitch_t)
    with_source = lambda i, value: put(second_t, at_step(i), value + y_rows(source_t)(i))
    solve_y(y_rows(field_t), held_t, with_source, False)

    solve_y(in_order(second_t), held_t, y_store(field_t), False)
    turn_back(field_t, field, planes, length_t, pitch_t, pitch)
    solve_z(field)
    x2 = start_x(x_rows(field), held, 1, False)
    finish_x(x2, held, x_store(field), 1, False)

    x3 = start_x(x_rows(field), held, 2, True)
    turn_over(field, final_t, planes, block, pitch, length_t)
    final_copies = send_blocks(final_t, 0)

    total = jnp.zeros((SUBLANES, columns), jnp.float32)
    for b in range(SUBLANES):
        for t in range(0, block, SUBLANES):
            value = take(field, slice(b * pitch + t, b * pitch + t + SUBLANES))
            total = total + value * value
    part_sum[me] = 0.5 * sum(total[:, j : j + LANES] for j in range(0, columns, LANES))
    misfit_copies = spread_out(part_sum, 5)

    finish_x(x3, held, x_store(field), 2, True)
    solve_z(field)
    turn_over(field, field_t, planes, block, pitch, pitch_t)
    solve_y(y_rows(field_t), held_t, lambda i, value: put(later_t, at_step(i), value), True)
    arrive(misfit_copies)
    sample_sum[own] = sum(part_sum[b] for b in range(parts))
    sample_copies = spread_samples(sample_sum, 0)

    solve_y(in_order(later_t), held_t, y_store(field_t), True)
    turn_back(field_t, field, planes, length_t, pitch_t, pitch)
    solve_z(field)
    x4 = start_x(x_rows(field), held, 3, True)
    half = lax.broadcasted_iota(jnp.int32, (block, LANES), 1) < block

    def assemble(phase, out):
        for j in range(parts // 2):
            for w in range(planes // 2):
                left = landed[phase, 2 * j, w]
                right = landed[phase, 2 * j + 1, w]
                cut = slice(j * LANES, (j + 1) * LANES)
                out[2 * w, :, cut] = jnp.where(half, left, pltpu.roll(right, block, 1))
                out[2 * w + 1, :, cut] = jnp.where(half, pltpu.roll(left, block, 1), right)

    arrive(final_copies)
    assemble(0, final_out)
    finish_x(x4, held, x_store(field), 3, True)
    turn_over(field, adjoint_t, planes, block, pitch, length_t)
    adjoint_copies = send_blocks(adjoint_t, 1)

    arrive(sample_copies)
    misfits = [jnp.sum(sample_sum[s], keepdims=True) for s in range(samples)]
    average = sum(misfits) / samples
    own_misfit = jnp.sum(sample_sum[own], keepdims=True)
    weight = (1.0 + aversion * (own_misfit - average) / (average + epsilon)) / samples
    picked = jnp.dot(
        take(adjoint_t, slice(None)), hits_x[...],
        precision=EXACT, preferred_element_type=jnp.float32) * hits_y[...]
    picked = picked + jnp.dot(
        take(later_t, slice(None)), hits_x[...],
        precision=EXACT, preferred_element_type=jnp.float32) * hits_step[...]
    picked = picked.reshape(grid_cells // SUBLANES, SUBLANES, picked.shape[1])
    term_sum[me] = weight * jnp.sum(picked, axis=0)
    term_copies = spread_out(term_sum, 6)
    arrive(term_copies)
    sample_term[own] = sum(term_sum[b] for b in range(parts))
    gradient_copies = spread_samples(sample_term, 1)
    arrive(gradient_copies)
    gradient_out[...] = jnp.sum(sum(sample_term[s] for s in range(samples)), axis=0, keepdims=True)

    arrive(adjoint_copies)
    assemble(1, adjoint_out)
    for copy in pending:
        copy.wait_send()


def fused(parts, samples, concentration, classes, conductivity, wells, control):
    _, planes, block, grid_cells = concentration.shape
    wide = planes * block
    count = wells.shape[1]
    f32 = jnp.float32
    vmem = lambda *shape: pltpu.VMEM(shape, f32)
    length_t = grid_cells // SUBLANES
    step = wide * grid_cells // block // SUBLANES
    flat = (step // LANES, SUBLANES * (block + 1), LANES)
    flat_even = (step // LANES, SUBLANES * block, LANES)
    turned = (wide // LANES, SUBLANES * (length_t + 1), LANES)
    turned_even = (wide // LANES, grid_cells, LANES)
    ordered = (step // LANES, block * SUBLANES, LANES)
    dma = pltpu.SemaphoreType.DMA
    scratch = [vmem(wide, grid_cells), pltpu.VMEM((wide, grid_cells), jnp.int32), dma((2,))]
    scratch += [vmem(*flat), vmem(*turned)]
    scratch += [vmem(*ordered)] * 5 + [vmem(*turned_even)] * 5 + [vmem(*flat_even)] * 2
    scratch += [vmem(*flat), vmem(*ordered), vmem(*turned), vmem(*turned_even)]
    scratch += [vmem(*turned_even)] * 2 + [vmem(*turned)] + [vmem(*turned_even)] * 2
    scratch += [
        vmem(wide, count), vmem(grid_cells, count), vmem(grid_cells, count),
        vmem(2, SUBLANES, step), vmem(2, SUBLANES, step),
        vmem(parts, 6 * SUBLANES, step),
        vmem(2, parts, 6 * SUBLANES, step),
        vmem(2, 12, SUBLANES, wide),
        vmem(4, parts, 2 * SUBLANES, step),
        vmem(parts + 1, SUBLANES, step), vmem(parts + 1, SUBLANES, step),
        vmem(2, parts, wide // LANES, block, LANES),
        vmem(parts, SUBLANES, LANES), vmem(samples, SUBLANES, LANES),
        vmem(parts, SUBLANES, count), vmem(samples, SUBLANES, count),
        dma((7, parts)), dma((7, parts)), dma((2, parts)), dma((2, parts)),
        dma((2, samples)), dma((2, samples)), dma((2,)), dma((2,)),
    ]
    on_vmem = pl.BlockSpec(memory_space=pltpu.VMEM)
    anywhere = pl.BlockSpec(memory_space=pltpu.HBM)
    on_smem = pl.BlockSpec(memory_space=pltpu.SMEM)
    out = jax.ShapeDtypeStruct((planes, block, grid_cells), f32)
    final, adjoint, gradient = pl.pallas_call(
        functools.partial(kernel, parts, samples, planes),
        out_shape=(out, out, jax.ShapeDtypeStruct((1, count), f32)),
        in_specs=[anywhere, anywhere, on_smem, on_vmem, on_vmem],
        out_specs=(on_vmem, on_vmem, on_vmem),
        scratch_shapes=scratch,
        compiler_params=pltpu.CompilerParams(
            collective_id=0, has_side_effects=True, vmem_limit_bytes=48 * 1024 * 1024),
    )(
        concentration.reshape(wide, grid_cells), classes.reshape(wide, grid_cells), conductivity, wells,
        control.reshape(1, count))
    return final[None], adjoint[None], gradient.reshape(count)


def choose(axes, concentration, classes, conductivity, wells, control):
    parts, samples = axes["space"], axes["sample"]
    _, planes, block, grid_cells = concentration.shape
    fits = (
        2 * block == LANES and planes % 2 == 0 and parts % 2 == 0 and parts > 1
        and parts * block == grid_cells and grid_cells % LANES == 0
        and (planes * block) % LANES == 0 and SUBLANES % planes == 0
        and (planes * grid_cells) % (SUBLANES * LANES) == 0 and grid_cells // SUBLANES == block
    )
    if fits:
        return fused(parts, samples, concentration, classes, conductivity, wells, control)
    return per_device(concentration, classes, conductivity, wells, control)


def solution(mesh):
    placed = (P("sample", None, "space", None), P("sample", None, "space", None), P(), P(), P())
    return jax.shard_map(
        functools.partial(choose, mesh.shape),
        mesh=mesh,
        in_specs=placed,
        out_specs=(P("sample", None, "space", None), P("sample", None, "space", None), P()),
        check_vma=False,
    )
```

```python
import functools
import jax
import jax.numpy as jnp
from jax import lax
from jax.experimental import pallas as pl
from jax.experimental.pallas import tpu as pltpu
from jax.sharding import PartitionSpec as P

spread_along = 200.0
drift_along = 6.0
spread_across = 200.0
drift_across = 3.0
spread_depth = 2.0
drift_depth = 0.0
aversion = 0.5
epsilon = 1e-06


def offset(values, amount, direction, filler):
    length = values.shape[direction]
    distance = abs(amount)
    margin = list(values.shape)
    margin[direction] = distance
    padding = jnp.full(margin, filler, values.dtype)
    if amount > 0:
        retained = lax.slice_in_dim(values, 0, length - distance, axis=direction)
        return jnp.concatenate([padding, retained], axis=direction)
    retained = lax.slice_in_dim(values, distance, length, axis=direction)
    return jnp.concatenate([retained, padding], axis=direction)


def line_terms(conduct, direction, spread, advection):
    following = offset(conduct, -1, direction, 0.0)
    face_ahead = 2.0 * conduct * following / (conduct + following)
    behind = offset(face_ahead, 1, direction, 0.0)
    subdiag = offset(-(spread * face_ahead + advection), 1, direction, 0.0)
    middle = 1.0 + spread * (behind + face_ahead) + advection
    superdiag = -spread * face_ahead
    return (subdiag, middle, superdiag)


def factor_lines(terms, direction):
    subdiag, middle, superdiag = terms
    length = middle.shape[direction]
    levels = []
    stride = 1
    while stride < length:
        middle_before = offset(middle, stride, direction, 1.0)
        middle_after = offset(middle, -stride, direction, 1.0)
        weight_below = -subdiag / middle_before
        weight_above = -superdiag / middle_after
        new_middle = (
            middle
            + weight_below * offset(superdiag, stride, direction, 0.0)
            + weight_above * offset(subdiag, -stride, direction, 0.0)
        )
        subdiag = weight_below * offset(subdiag, stride, direction, 0.0)
        superdiag = weight_above * offset(superdiag, -stride, direction, 0.0)
        middle = new_middle
        levels.append((weight_below, weight_above))
        stride = stride * 2
    return (levels, middle)


def solve_lines(values, factored, direction):
    levels, middle = factored
    stride = 1
    for weight_below, weight_above in levels:
        values = (
            values
            + weight_below * offset(values, stride, direction, 0.0)
            + weight_above * offset(values, -stride, direction, 0.0)
        )
        stride = stride * 2
    return values / middle


def solve_back(values, factored, direction):
    levels, middle = factored
    values = values / middle
    for depth_level in range(len(levels) - 1, -1, -1):
        weight_below, weight_above = levels[depth_level]
        stride = 2**depth_level
        values = (
            values
            + offset(weight_below * values, -stride, direction, 0.0)
            + offset(weight_above * values, stride, direction, 0.0)
        )
    return values


def pack_lines(values):
    planes, rows_here, length = values.shape
    count = lax.axis_size("space")
    return values.reshape(planes, rows_here, count, length // count).transpose(0, 2, 3, 1)


def unpack_lines(values):
    return values.reshape(values.shape[0], values.shape[2], values.shape[3])


def into_columns(values):
    return unpack_lines(
        lax.all_to_all(pack_lines(values), "space", split_axis=1, concat_axis=3, tiled=True)
    )


def into_rows(values):
    return unpack_lines(
        lax.all_to_all(pack_lines(values), "space", split_axis=1, concat_axis=3, tiled=True)
    )


def well_sum(column_sum, hits_rows, hits_columns):
    picked = jnp.dot(
        hits_rows, column_sum, precision=lax.Precision.HIGHEST, preferred_element_type=jnp.float32
    )
    return jnp.sum(picked * hits_columns, axis=1)


def per_device(concentration, classes, conductivity, wells, control):
    start_state = concentration[0]
    class_cells = classes[0]
    grid_cells = start_state.shape[2]
    block_size = start_state.shape[1]
    position = lax.axis_index("space")
    conduct_rows = jnp.zeros(class_cells.shape, jnp.float32)
    for class_label in range(conductivity.shape[0]):
        conduct_rows = conduct_rows + jnp.where(
            class_cells == class_label, conductivity[class_label], 0.0
        )
    conduct_columns = unpack_lines(
        lax.all_to_all(pack_lines(conduct_rows), "space", split_axis=1, concat_axis=3, tiled=True)
    )
    along_factor = factor_lines(line_terms(conduct_columns, 2, spread_along, drift_along), 2)
    across_factor = factor_lines(line_terms(conduct_rows, 2, spread_across, drift_across), 2)
    depth_rows = factor_lines(line_terms(conduct_rows, 0, spread_depth, drift_depth), 0)
    local_index = position * block_size + lax.iota(jnp.int32, block_size)
    all_index = lax.iota(jnp.int32, grid_cells)
    hits_first_local = (wells[0][:, None] == local_index[None, :]).astype(jnp.float32)
    hits_second_all = (wells[1][:, None] == all_index[None, :]).astype(jnp.float32)
    hits_second_local = (wells[1][:, None] == local_index[None, :]).astype(jnp.float32)
    hits_first_all = (wells[0][:, None] == all_index[None, :]).astype(jnp.float32)
    source = jnp.dot(
        hits_first_local.T,
        control[:, None] * hits_second_all,
        precision=lax.Precision.HIGHEST,
        preferred_element_type=jnp.float32,
    )
    depth_columns = factor_lines(line_terms(conduct_columns, 0, spread_depth, drift_depth), 0)
    current = into_columns(start_state + source[None])
    current = solve_lines(current, along_factor, 2)
    current = solve_lines(current, depth_columns, 0)
    current = into_rows(current)
    current = solve_lines(current, across_factor, 2)
    current = current + source[None]
    current = solve_lines(current, across_factor, 2)
    current = solve_lines(current, depth_rows, 0)
    final_state = solve_lines(into_columns(current), along_factor, 2)
    misfit_part = 0.5 * jnp.sum(final_state * final_state)
    second_adjoint = solve_back(final_state, along_factor, 2)
    second_adjoint = solve_back(second_adjoint, depth_columns, 0)
    second_adjoint = solve_back(into_rows(second_adjoint), across_factor, 2)
    first_adjoint = solve_back(second_adjoint, across_factor, 2)
    first_adjoint = solve_back(first_adjoint, depth_rows, 0)
    adjoint_state = solve_back(into_columns(first_adjoint), along_factor, 2)
    well_terms = well_sum(jnp.sum(second_adjoint, axis=0), hits_first_local, hits_second_all)
    well_terms = well_terms + well_sum(
        jnp.sum(adjoint_state, axis=0), hits_second_local, hits_first_all
    )
    sample_count = lax.axis_size("sample")
    own_misfit = lax.psum(misfit_part, "space")
    misfit_total = lax.psum(own_misfit, "sample")
    average = misfit_total / sample_count
    weight = (1.0 + aversion * (own_misfit - average) / (average + epsilon)) / sample_count
    gradient = lax.psum(weight * well_terms, ("sample", "space"))
    return (final_state[None], adjoint_state[None], gradient)


LANES = 128
SUBLANES = 8
UNROLL = 8
TURN = 16
MESH = pl.DeviceIdType.MESH
EXACT = lax.Precision.HIGHEST


def inverse(x):
    r = pl.reciprocal(x, approx=True)
    r = r * (2.0 - x * r)
    return r * (2.0 - x * r)


def steps(count, load, work, store, carry):
    def turn(t, state):
        waiting = []
        for first in range(0, TURN, UNROLL):
            group = [t * TURN + first + k for k in range(UNROLL)]
            loaded = [load(i) for i in group]
            for i, result in waiting:
                store(i, result)
            waiting = []
            for i, values in zip(group, loaded):
                state, result = work(i, state, values)
                waiting.append((i, result))
        for i, result in waiting:
            store(i, result)
        return state

    return lax.fori_loop(0, count // TURN, turn, carry)


def at_step(i):
    return pl.ds(pl.multiple_of(i * SUBLANES, SUBLANES), SUBLANES)


def gather_rows(ref, i, pitch):
    return take(ref, pl.ds(i, SUBLANES, stride=pitch))


def scatter_rows(ref, i, pitch, value):
    put(ref, pl.ds(i, SUBLANES, stride=pitch), value)


def take(ref, at):
    return jnp.concatenate([ref[j, at, :] for j in range(ref.shape[0])], axis=1)


def put(ref, at, value):
    for j in range(ref.shape[0]):
        ref[j, at, :] = value[:, j * LANES : (j + 1) * LANES]


def width(ref):
    return ref.shape[0] * LANES


def factor_blocks(lines, length):
    def load(i):
        return [line[0](jnp.minimum(i + 1, length - 1)) for line in lines]

    def work(i, states, loaded):
        new_states, results = [], []
        for (_, _, _, last_face, spread, drift), state, after in zip(lines, states, loaded):
            here, behind, u, eta, eta_t, corner = state
            ahead = 2.0 * here * after * inverse(here + after)
            ahead = jnp.where(i == length - 1, last_face, ahead)
            r = inverse(1.0 + spread * (behind + ahead) + drift + (spread * behind + drift) * u)
            u = -spread * ahead * r
            lo = -(spread * ahead + drift) * r
            first = eta * r
            new_states.append((after, ahead, u, -lo * eta, -u * eta_t, corner + first * eta_t))
            results.append((lo, u, r, first, eta_t * r))
        return new_states, results

    def store(i, results):
        for line, result in zip(lines, results):
            for ref, value in zip(line[1], result):
                put(ref, at_step(i), value)

    start = []
    for read, factors, before, _, _, _ in lines:
        ones = jnp.ones((SUBLANES, width(factors[0])), jnp.float32)
        zeros = jnp.zeros_like(ones)
        start.append((read(0), before, zeros, ones, ones, zeros))
    states = steps(length, load, work, store, start)
    at = at_step(length - 1)
    corners = []
    for line, state in zip(lines, states):
        _, _, inv, from_first, to_first = line[1]
        corners.append((state[5], take(from_first, at), take(to_first, at), take(inv, at)))
    return corners


def sweep_down(read, out, low, inv, weights, length):
    def load(i):
        at = at_step(i)
        return read(i), take(inv, at), take(low, at), take(weights, at)

    def work(i, state, values):
        y, lo, total = state
        here, r, lo_next, share = values
        y = here - lo * y
        return (y, lo_next, total + share * y), y * r

    def store(i, z):
        put(out, at_step(i), z)

    zeros = jnp.zeros((SUBLANES, width(low)), jnp.float32)
    _, _, total = steps(length, load, work, store, (zeros, zeros, zeros))
    return total, take(out, at_step(length - 1))


def sweep_up(held, write, up, spike, incoming, following, length):
    def load(k):
        at = at_step(length - 1 - k)
        return take(held, at), take(spike, at), take(up, at)

    def work(k, x, values):
        here, share, factor = values
        x = here - share * incoming - factor * x
        return x, x

    def store(k, x):
        write(length - 1 - k, x)

    steps(length, load, work, store, following)


def joint_terms(vf, vl, wf, wl, beta):
    r = inverse(1.0 - vf * beta)
    s = vl * beta * r
    return s, vl + s * vf, r, r * vf, r * wf, wl + s * wf


def turn_over(source, target, planes, length, pitch, pitch_to):
    tiles = source.shape[0]
    for i in range(target.shape[0]):
        for j in range(target.shape[1] // pitch_to // 2):
            first = j // tiles * planes + 2 * i
            tile = jnp.concatenate(
                [source[j % tiles, b * pitch : b * pitch + length, :] for b in (first, first + 1)],
                axis=0).T
            for half in range(2):
                start = (2 * j + half) * pitch_to
                target[i, start : start + length, :] = tile[half * length : (half + 1) * length, :]


def turn_back(source, target, planes, length, pitch, pitch_to):
    tiles = target.shape[0]
    for i in range(source.shape[0]):
        for j in range(source.shape[1] // pitch // 2):
            tile = jnp.concatenate(
                [source[i, b * pitch : b * pitch + length, :] for b in (2 * j, 2 * j + 1)], axis=0).T
            for half in range(2):
                start = (j // tiles * planes + 2 * i + half) * pitch_to
                target[j % tiles, start : start + length, :] = tile[
                    half * length : (half + 1) * length, :]


def kernel(
    parts, samples, planes,
    conc_in, classes_in, conductivity, wells, control,
    final_out, adjoint_out, gradient_out,
    conc, classes, in_sem, cond, cond_t, xl, xu, xi, xe, xf, yl, yu, yi, ye, yf, zu, zi,
    field, held, field_t, held_t, second_t, later_t, source_t, final_t, adjoint_t,
    hits_x, hits_y, hits_step, halo_send, halo, corner, joint_x, joint_y, ends, ps, qs,
    landed, part_sum, sample_sum, term_sum, sample_term,
    send_sem, recv_sem, bulk_send, bulk_recv, sample_send, sample_recv, halo_ssem, halo_rsem,
):
    me = lax.axis_index("space")
    own = lax.axis_index("sample")
    block = conc.shape[0] // planes
    grid_cells = conc.shape[1]
    length_t = grid_cells // SUBLANES
    wide = conc.shape[0]
    pitch, pitch_t = block + 1, length_t + 1
    class_copy = pltpu.make_async_copy(classes_in, classes, in_sem.at[0])
    class_copy.start()
    conc_copy = pltpu.make_async_copy(conc_in, conc, in_sem.at[1])
    conc_copy.start()

    barrier = pltpu.get_barrier_semaphore()

    def peer(k):
        return {"space": lax.rem(me + k, parts)}

    def partner(k):
        return {"sample": lax.rem(own + k, samples)}

    for k in range(1, parts):
        pl.semaphore_signal(barrier, inc=1, device_id=peer(k), device_id_type=MESH)
    for k in range(1, samples):
        pl.semaphore_signal(barrier, inc=1, device_id=partner(k), device_id_type=MESH)

    def spread_out(ref, phase):
        copies = []
        for k in range(1, parts):
            copy = pltpu.make_async_remote_copy(
                src_ref=ref.at[me], dst_ref=ref.at[me],
                send_sem=send_sem.at[phase, k], recv_sem=recv_sem.at[phase, k],
                device_id=peer(k), device_id_type=MESH)
            copy.start()
            copies.append(copy)
        return copies

    def spread_samples(ref, phase):
        copies = []
        for k in range(1, samples):
            copy = pltpu.make_async_remote_copy(
                src_ref=ref.at[own], dst_ref=ref.at[own],
                send_sem=sample_send.at[phase, k], recv_sem=sample_recv.at[phase, k],
                device_id=partner(k), device_id_type=MESH)
            copy.start()
            copies.append(copy)
        return copies

    def send_blocks(ref, phase):
        copies = []
        for k in range(1, parts):
            to = lax.rem(me + k, parts)
            copy = pltpu.make_async_remote_copy(
                src_ref=ref.at[:, pl.ds(pl.multiple_of(to * block, block), block)],
                dst_ref=landed.at[phase, me],
                send_sem=bulk_send.at[phase, k], recv_sem=bulk_recv.at[phase, k],
                device_id=peer(k), device_id_type=MESH)
            copy.start()
            copies.append(copy)
        landed[phase, me] = ref[:, pl.ds(pl.multiple_of(me * block, block), block), :]
        return copies

    pending = []

    def arrive(copies):
        for copy in copies:
            copy.wait_recv()
        pending.extend(copies)

    class_copy.wait()

    def x_rows(ref):
        return lambda i: gather_rows(ref, i, pitch)

    def x_store(ref):
        return lambda i, value: scatter_rows(ref, i, pitch, value)

    def y_rows(ref):
        return lambda i: gather_rows(ref, i, pitch_t)

    def y_store(ref):
        return lambda i, value: scatter_rows(ref, i, pitch_t, value)

    def in_order(ref):
        return lambda i: take(ref, at_step(i))

    groups = SUBLANES // planes
    columns = grid_cells // groups
    for g in range(groups):
        for z in range(planes):
            for t in range(0, block, SUBLANES):
                start = z * block + t
                labels = classes[start : start + SUBLANES, g * columns : (g + 1) * columns]
                values = jnp.full(labels.shape, conductivity[0], jnp.float32)
                for label in range(1, conductivity.shape[0]):
                    values = jnp.where(labels == label, conductivity[label], values)
                start = (g * planes + z) * pitch + t
                put(cond, slice(start, start + SUBLANES), values)
    x_cond = x_rows(cond)
    halo_send[0] = x_cond(block - 1)
    halo_send[1] = x_cond(0)
    pl.semaphore_wait(barrier, parts - 1 + samples - 1)
    halo_copies = []
    for side, k in ((0, 1), (1, parts - 1)):
        copy = pltpu.make_async_remote_copy(
            src_ref=halo_send.at[side], dst_ref=halo.at[side],
            send_sem=halo_ssem.at[side], recv_sem=halo_rsem.at[side],
            device_id=peer(k), device_id_type=MESH)
        copy.start()
        halo_copies.append(copy)

    turn_over(cond, cond_t, planes, block, pitch, pitch_t)

    x_row = lax.broadcasted_iota(jnp.int32, hits_x.shape, 0) % block + me * block
    hits_x[...] = jnp.where(x_row == wells[0:1, :], 1.0, 0.0)
    y_row = lax.broadcasted_iota(jnp.int32, hits_y.shape, 0)
    hits_y[...] = jnp.where(y_row == wells[1:2, :], 1.0, 0.0)
    y_row = y_row % SUBLANES * length_t + y_row // SUBLANES
    hits_step[...] = jnp.where(y_row == wells[1:2, :], 1.0, 0.0)
    across_last = (((1,), (1,)), ((), ()))
    source = lax.dot_general(
        hits_x[0:block, :] * control[...], hits_y[...], across_last,
        precision=EXACT, preferred_element_type=jnp.float32)
    conc_copy.wait()
    for g in range(groups):
        cut = slice(g * columns, (g + 1) * columns)
        for z in range(planes):
            start = (g * planes + z) * pitch
            put(field, slice(start, start + block),
                conc[z * block : (z + 1) * block, cut] + source[:, cut])

    row = lax.broadcasted_iota(jnp.int32, (SUBLANES, wide), 0)
    y_factors = (yl, yu, yi, ye, yf)
    y_cond = y_rows(cond_t)
    y_first = y_cond(0)
    y_last = y_cond(length_t - 1)
    last_before = pltpu.roll(y_last, 1, 0)
    y_before = jnp.where(row == 0, 0.0, 2.0 * last_before * y_first / (last_before + y_first))

    first_after = pltpu.roll(y_first, SUBLANES - 1, 0)
    y_ahead = jnp.where(row == SUBLANES - 1, 0.0, 2.0 * y_last * first_after / (y_last + first_after))

    arrive(halo_copies)
    x_factors = (xl, xu, xi, xe, xf)
    not_first = (me > 0).astype(jnp.float32)
    not_last = (me < parts - 1).astype(jnp.float32)
    first_row = x_cond(0)
    face_before = not_first * 2.0 * halo[0] * first_row / (halo[0] + first_row)

    last_row = x_cond(block - 1)
    face_ahead = not_last * 2.0 * halo[1] * last_row / (halo[1] + last_row)
    (gff, glf, gfl, gll), y_corners = factor_blocks(
        (
            (x_cond, x_factors, face_before, face_ahead, spread_along, drift_along),
            (y_cond, y_factors, y_before, y_ahead, spread_across, drift_across),
        ), block)
    for j, value in enumerate((gff, glf, gfl, gll, face_before, face_ahead)):
        corner[me, j * SUBLANES : (j + 1) * SUBLANES, :] = value
    corner_copies = spread_out(corner, 0)

    def ends_out(phase, first, last):
        ends[phase, me, 0:SUBLANES, :] = first
        ends[phase, me, SUBLANES : 2 * SUBLANES, :] = last
        copies = []
        for k in range(1, parts):
            copy = pltpu.make_async_remote_copy(
                src_ref=ends.at[phase, me], dst_ref=ends.at[phase, me],
                send_sem=send_sem.at[phase + 1, k], recv_sem=recv_sem.at[phase + 1, k],
                device_id=peer(k), device_id_type=MESH)
            copy.start()
            copies.append(copy)
        return copies

    def start_x(read, out, phase, flipped):
        low, weights = (xu, xe) if flipped else (xl, xf)
        first, last = sweep_down(read, out, low, xi, weights, block)
        return ends_out(phase, first, last)

    def finish_x(copies, inner, write, phase, flipped):
        arrive(copies)
        way = 1 if flipped else 0
        joint = lambda b, j: joint_x[way, b, j * SUBLANES : (j + 1) * SUBLANES, :]
        firsts = [ends[phase, b, 0:SUBLANES, :] for b in range(parts)]
        alphas = []
        alpha = None
        for b in range(parts):
            last = ends[phase, b, SUBLANES : 2 * SUBLANES, :]
            alpha = last if b == 0 else last + joint(b, 0) * firsts[b] - joint(b, 1) * alpha
            alphas.append(alpha)
        zero = jnp.zeros_like(firsts[0])
        ps[parts] = zero
        qs[0] = zero
        p = zero
        for b in range(parts - 1, -1, -1):
            if b < parts - 1:
                qs[b + 1] = alphas[b] - joint(b, 5) * p
            value = joint(b, 2) * firsts[b] - joint(b, 4) * p
            if b > 0:
                value = value - joint(b, 3) * alphas[b - 1]
            p = value
            ps[b] = p
        coupling = -spread_along * face_before if flipped else -(spread_along * face_before + drift_along)
        incoming = coupling * qs[me]
        up, spike = (xl, xf) if flipped else (xu, xe)
        sweep_up(inner, write, up, spike, incoming, ps[me + 1], block)

    x1 = start_x(x_rows(field), held, 0, False)

    for g, t in [(g, t) for g in range(groups) for t in range(0, block, SUBLANES)]:
        start = g * planes * pitch + t
        here = take(cond, slice(start, start + SUBLANES))
        behind = jnp.zeros(here.shape, jnp.float32)
        u = behind
        for z in range(planes):
            if z < planes - 1:
                start = (g * planes + z + 1) * pitch + t
                after = take(cond, slice(start, start + SUBLANES))
                ahead = 2.0 * here * after * inverse(here + after)
            else:
                after, ahead = here, jnp.zeros(here.shape, jnp.float32)
            r = inverse(1.0 + spread_depth * (behind + ahead) + spread_depth * behind * u)
            u = -spread_depth * ahead * r
            start = (g * planes + z) * block + t
            put(zi, slice(start, start + SUBLANES), r)
            put(zu, slice(start, start + SUBLANES), u)
            here, behind = after, ahead

    gff, glf, gfl, gll = y_corners
    y_couplings = []
    for way in range(2):
        a = jnp.where(row == 0, 0.0, -(spread_across * y_before + drift_across))
        a_next = jnp.where(row == SUBLANES - 1, 0.0, -(spread_across * y_ahead + drift_across))
        c = -spread_across * y_before
        c_next = -spread_across * y_ahead
        if way == 0:
            vf, vl, wf, wl = a * gff, a * glf, c_next * gfl, c_next * gll
            y_couplings.append(a)
        else:
            vf, vl, wf, wl = c * gff, c * gfl, a_next * glf, a_next * gll
            y_couplings.append(c)
        beta = jnp.zeros((1, wide), jnp.float32)
        for b in range(SUBLANES):
            cut = slice(b, b + 1)
            terms = joint_terms(vf[cut], vl[cut], wf[cut], wl[cut], beta)
            beta = terms[5]
            for j, value in enumerate(terms):
                joint_y[way, j, b : b + 1, :] = value
        ahead = jnp.where(row == 0, 0.0, -joint_y[way, 1])
        back = -joint_y[way, 4]
        back = jnp.where(row == SUBLANES - 1, 0.0, back)
        for level, distance in enumerate((1, 2, 4)):
            joint_y[way, 6 + level] = ahead
            joint_y[way, 9 + level] = back
            ahead = jnp.where(row < 2 * distance, 0.0, ahead * pltpu.roll(ahead, distance, 0))
            back = jnp.where(
                row >= SUBLANES - 2 * distance, 0.0,
                back * pltpu.roll(back, SUBLANES - distance, 0))

    def solve_y(read, inner, write, flipped):
        way = 1 if flipped else 0
        low, weights = (yu, ye) if flipped else (yl, yf)
        up, spike = (yl, yf) if flipped else (yu, ye)
        first, last = sweep_down(read, inner, low, yi, weights, length_t)
        alpha = last + joint_y[way, 0] * first
        for level, distance in enumerate((1, 2, 4)):
            alpha = alpha + joint_y[way, 6 + level] * pltpu.roll(alpha, distance, 0)
        alpha_before = jnp.where(row == 0, 0.0, pltpu.roll(alpha, 1, 0))
        p = joint_y[way, 2] * first - joint_y[way, 3] * alpha_before
        for level, distance in enumerate((1, 2, 4)):
            p = p + joint_y[way, 9 + level] * pltpu.roll(p, SUBLANES - distance, 0)
        p_next = jnp.where(row == SUBLANES - 1, 0.0, pltpu.roll(p, SUBLANES - 1, 0))
        q = alpha - joint_y[way, 5] * p_next
        q_before = jnp.where(row == 0, 0.0, pltpu.roll(q, 1, 0))
        incoming = y_couplings[way] * q_before
        sweep_up(inner, write, up, spike, incoming, p_next, length_t)

    def solve_z(values):
        for g, t in [(g, t) for g in range(groups) for t in range(0, block, SUBLANES)]:
            ats = [(g * planes + z) * block + t for z in range(planes)]
            cells = [(g * planes + z) * pitch + t for z in range(planes)]
            ats = [slice(start, start + SUBLANES) for start in ats]
            cells = [slice(start, start + SUBLANES) for start in cells]
            ys = [take(values, cells[0])]
            us = [take(zu, at) for at in ats]
            for z in range(1, planes):
                ys.append(take(values, cells[z]) - us[z - 1] * ys[-1])
            x = ys[-1] * take(zi, ats[-1])
            put(values, cells[-1], x)
            for z in range(planes - 2, -1, -1):
                x = ys[z] * take(zi, ats[z]) - us[z] * x
                put(values, cells[z], x)

    source_turned = lax.dot_general(
        hits_y[...] * control[...], hits_x[...], across_last,
        precision=EXACT, preferred_element_type=jnp.float32)
    for b in range(SUBLANES):
        put(source_t, slice(b * pitch_t, b * pitch_t + length_t),
            source_turned[b * length_t : (b + 1) * length_t, :])

    arrive(corner_copies)
    corner_of = lambda b, j: corner[b, j * SUBLANES : (j + 1) * SUBLANES, :]
    for way in range(2):
        beta = jnp.zeros((SUBLANES, corner.shape[2]), jnp.float32)
        for b in range(parts):
            gff, glf, gfl, gll, behind, ahead = [corner_of(b, j) for j in range(6)]
            a = -(spread_along * behind + drift_along) if b > 0 else jnp.zeros_like(behind)
            a_next = -(spread_along * ahead + drift_along) if b < parts - 1 else jnp.zeros_like(ahead)
            c, c_next = -spread_along * behind, -spread_along * ahead
            if way == 0:
                terms = joint_terms(a * gff, a * glf, c_next * gfl, c_next * gll, beta)
            else:
                terms = joint_terms(c * gff, c * gfl, a_next * glf, a_next * gll, beta)
            beta = terms[5]
            for j, value in enumerate(terms):
                joint_x[way, b, j * SUBLANES : (j + 1) * SUBLANES, :] = value

    finish_x(x1, held, x_store(field), 0, False)
    solve_z(field)
    turn_over(field, field_t, planes, block, pitch, pitch_t)
    with_source = lambda i, value: put(second_t, at_step(i), value + y_rows(source_t)(i))
    solve_y(y_rows(field_t), held_t, with_source, False)

    solve_y(in_order(second_t), held_t, y_store(field_t), False)
    turn_back(field_t, field, planes, length_t, pitch_t, pitch)
    solve_z(field)
    x2 = start_x(x_rows(field), held, 1, False)
    finish_x(x2, held, x_store(field), 1, False)

    x3 = start_x(x_rows(field), held, 2, True)
    turn_over(field, final_t, planes, block, pitch, length_t)
    final_copies = send_blocks(final_t, 0)

    total = jnp.zeros((SUBLANES, columns), jnp.float32)
    for b in range(SUBLANES):
        for t in range(0, block, SUBLANES):
            value = take(field, slice(b * pitch + t, b * pitch + t + SUBLANES))
            total = total + value * value
    part_sum[me] = 0.5 * sum(total[:, j : j + LANES] for j in range(0, columns, LANES))
    misfit_copies = spread_out(part_sum, 5)

    finish_x(x3, held, x_store(field), 2, True)
    solve_z(field)
    turn_over(field, field_t, planes, block, pitch, pitch_t)
    solve_y(y_rows(field_t), held_t, lambda i, value: put(later_t, at_step(i), value), True)
    arrive(misfit_copies)
    sample_sum[own] = sum(part_sum[b] for b in range(parts))
    sample_copies = spread_samples(sample_sum, 0)

    solve_y(in_order(later_t), held_t, y_store(field_t), True)
    turn_back(field_t, field, planes, length_t, pitch_t, pitch)
    solve_z(field)
    x4 = start_x(x_rows(field), held, 3, True)
    half = lax.broadcasted_iota(jnp.int32, (block, LANES), 1) < block

    def assemble(phase, out):
        for j in range(parts // 2):
            for w in range(planes // 2):
                left = landed[phase, 2 * j, w]
                right = landed[phase, 2 * j + 1, w]
                cut = slice(j * LANES, (j + 1) * LANES)
                out[2 * w, :, cut] = jnp.where(half, left, pltpu.roll(right, block, 1))
                out[2 * w + 1, :, cut] = jnp.where(half, pltpu.roll(left, block, 1), right)

    arrive(final_copies)
    assemble(0, final_out)
    finish_x(x4, held, x_store(field), 3, True)
    turn_over(field, adjoint_t, planes, block, pitch, length_t)
    adjoint_copies = send_blocks(adjoint_t, 1)

    arrive(sample_copies)
    misfits = [jnp.sum(sample_sum[s], keepdims=True) for s in range(samples)]
    average = sum(misfits) / samples
    own_misfit = jnp.sum(sample_sum[own], keepdims=True)
    weight = (1.0 + aversion * (own_misfit - average) / (average + epsilon)) / samples
    picked = jnp.dot(
        take(adjoint_t, slice(None)), hits_x[...],
        precision=EXACT, preferred_element_type=jnp.float32) * hits_y[...]
    picked = picked + jnp.dot(
        take(later_t, slice(None)), hits_x[...],
        precision=EXACT, preferred_element_type=jnp.float32) * hits_step[...]
    picked = picked.reshape(grid_cells // SUBLANES, SUBLANES, picked.shape[1])
    term_sum[me] = weight * jnp.sum(picked, axis=0)
    term_copies = spread_out(term_sum, 6)
    arrive(term_copies)
    sample_term[own] = sum(term_sum[b] for b in range(parts))
    gradient_copies = spread_samples(sample_term, 1)
    arrive(gradient_copies)
    gradient_out[...] = jnp.sum(sum(sample_term[s] for s in range(samples)), axis=0, keepdims=True)

    arrive(adjoint_copies)
    assemble(1, adjoint_out)
    for copy in pending:
        copy.wait_send()


def fused(parts, samples, concentration, classes, conductivity, wells, control):
    _, planes, block, grid_cells = concentration.shape
    wide = planes * block
    count = wells.shape[1]
    f32 = jnp.float32
    vmem = lambda *shape: pltpu.VMEM(shape, f32)
    length_t = grid_cells // SUBLANES
    step = wide * grid_cells // block // SUBLANES
    flat = (step // LANES, SUBLANES * (block + 1), LANES)
    flat_even = (step // LANES, SUBLANES * block, LANES)
    turned = (wide // LANES, SUBLANES * (length_t + 1), LANES)
    turned_even = (wide // LANES, grid_cells, LANES)
    ordered = (step // LANES, block * SUBLANES, LANES)
    dma = pltpu.SemaphoreType.DMA
    scratch = [vmem(wide, grid_cells), pltpu.VMEM((wide, grid_cells), jnp.int32), dma((2,))]
    scratch += [vmem(*flat), vmem(*turned)]
    scratch += [vmem(*ordered)] * 5 + [vmem(*turned_even)] * 5 + [vmem(*flat_even)] * 2
    scratch += [vmem(*flat), vmem(*ordered), vmem(*turned), vmem(*turned_even)]
    scratch += [vmem(*turned_even)] * 2 + [vmem(*turned)] + [vmem(*turned_even)] * 2
    scratch += [
        vmem(wide, count), vmem(grid_cells, count), vmem(grid_cells, count),
        vmem(2, SUBLANES, step), vmem(2, SUBLANES, step),
        vmem(parts, 6 * SUBLANES, step),
        vmem(2, parts, 6 * SUBLANES, step),
        vmem(2, 12, SUBLANES, wide),
        vmem(4, parts, 2 * SUBLANES, step),
        vmem(parts + 1, SUBLANES, step), vmem(parts + 1, SUBLANES, step),
        vmem(2, parts, wide // LANES, block, LANES),
        vmem(parts, SUBLANES, LANES), vmem(samples, SUBLANES, LANES),
        vmem(parts, SUBLANES, count), vmem(samples, SUBLANES, count),
        dma((7, parts)), dma((7, parts)), dma((2, parts)), dma((2, parts)),
        dma((2, samples)), dma((2, samples)), dma((2,)), dma((2,)),
    ]
    on_vmem = pl.BlockSpec(memory_space=pltpu.VMEM)
    anywhere = pl.BlockSpec(memory_space=pltpu.HBM)
    on_smem = pl.BlockSpec(memory_space=pltpu.SMEM)
    out = jax.ShapeDtypeStruct((planes, block, grid_cells), f32)
    final, adjoint, gradient = pl.pallas_call(
        functools.partial(kernel, parts, samples, planes),
        out_shape=(out, out, jax.ShapeDtypeStruct((1, count), f32)),
        in_specs=[anywhere, anywhere, on_smem, on_vmem, on_vmem],
        out_specs=(on_vmem, on_vmem, on_vmem),
        scratch_shapes=scratch,
        compiler_params=pltpu.CompilerParams(
            collective_id=0, has_side_effects=True, vmem_limit_bytes=63 * 1024 * 1024),
    )(
        concentration.reshape(wide, grid_cells), classes.reshape(wide, grid_cells), conductivity, wells,
        control.reshape(1, count))
    return final[None], adjoint[None], gradient.reshape(count)


def choose(axes, concentration, classes, conductivity, wells, control):
    parts, samples = axes["space"], axes["sample"]
    _, planes, block, grid_cells = concentration.shape
    fits = (
        2 * block == LANES and planes % 2 == 0 and parts % 2 == 0 and parts > 1
        and parts * block == grid_cells and grid_cells % LANES == 0
        and (planes * block) % LANES == 0 and SUBLANES % planes == 0
        and (planes * grid_cells) % (SUBLANES * LANES) == 0 and grid_cells // SUBLANES == block
    )
    if fits:
        return fused(parts, samples, concentration, classes, conductivity, wells, control)
    return per_device(concentration, classes, conductivity, wells, control)


def solution(mesh):
    placed = (P("sample", None, "space", None), P("sample", None, "space", None), P(), P(), P())
    return jax.shard_map(
        functools.partial(choose, mesh.shape),
        mesh=mesh,
        in_specs=placed,
        out_specs=(P("sample", None, "space", None), P("sample", None, "space", None), P()),
        check_vma=False,
    )
```
